256 devices in a mesh: depth: 16 (over z_hi, x), height: 2 (over z_lo), batch: 8 (over y, core).
Axes of the slice: x: 4, y: 4, z: 8 (z_hi: 4, z_lo: 2; z = z_hi * 2 + z_lo), core: 2. Of those that a mesh axis runs over, the one named last changes fastest.
Arguments:
- volume: bfloat16 [8, 224, 28, 14, 384], P('batch', 'depth', 'height'), may hold values from -6 to 6
- patch_mask: int32 [8, 224, 28, 14], P('batch', 'depth', 'height'), may hold values 0 or 1
- mask_token: bfloat16 [384], replicated, may hold values from -4 to 4
- labels: int32 [8, 224, 28, 14], P('batch', 'depth', 'height'), may hold values from 0 to 3
- norm_gain: float32 [384], replicated, may hold values from 0.1 to 1.9
- qkv_weight: bfloat16 [384, 576], replicated, may hold values from -2 to 2
- proj_weight: bfloat16 [192, 384], replicated, may hold values from -0.4375 to 0.4375
- merge_gain: float32 [3072], replicated, may hold values from 0.1 to 1.9
- merge_weight: bfloat16 [3072, 768], P(None, 'height'), may hold values from -0.109375 to 0.109375
- upstream: bfloat16 [8, 224, 28, 14, 384], P('batch', 'depth', 'height'), may hold values from -6 to 6
Outputs:
- merged: bfloat16 [8, 112, 14, 7, 768], P('batch', 'depth', None, None, 'height')
- grad_qkv: float32 [384, 576], P(('depth', 'height'))
- grad_proj: float32 [192, 384], P(('depth', 'height'))
The draws below stay inside these ranges and needn't reach their ends.
All inputs are finite; a program needn't handle non-finite values. No bound on the sum of `patch_mask` on one device may be relied on, other than what follows from the above.
Results may differ from the reference program's by a relative error of at most 0.034.
The reference program's roundings to bfloat16 on the way count: a program that leaves them out, or rounds other values in their place, can miss the bound.
Values may be sent and summed in bfloat16 or wider, within the bound.
A program may use at most 128 MiB of HBM per device.

```python
import jax
import jax.numpy as jnp
from jax import lax

C = 384
HEADS = 6
ATTN = 192
WIN = 7
SHIFT = 3
WIDE = 14
BATCH = 8
DEPTH = 224
HEIGHT = 28


def draw_qkv_weight(key, part):
    key = jax.random.fold_in(key, 11)
    entries = jnp.clip(jax.random.normal(key, (C, 3 * ATTN), jnp.float32), -6.0, 6.0) * C ** (-0.5)
    return entries.astype(jnp.bfloat16)


def with_ends(array, own_key, least, high):
    longest = array.shape.index(max(array.shape))
    spots = []
    for shift in (0, 1):
        where = [jax.random.randint(jax.random.fold_in(own_key, axis), (), 0, length) for axis, length in enumerate(array.shape)]
        where[longest] = (where[longest] + shift) % array.shape[longest]
        spots.append(tuple(where))
    return array.at[spots[0]].set(least).at[spots[1]].set(high)


def block_levels(own_key, extent, cuts, smallest, top_value):
    def one(position, shards_of):
        draws = jax.random.uniform(jax.random.fold_in(jax.random.fold_in(own_key, 6), position), (shards_of,), jnp.float32, smallest / len(cuts), top_value / len(cuts))
        return jnp.repeat(jnp.exp(draws), extent[position] // shards_of).reshape((-1,) + (1,) * (len(extent) - position - 1))

    gain = one(*cuts[0])
    for cut in cuts[1:]:
        gain = gain * one(*cut)
    return gain


def centred(key, shape, scale, reach, split=(), kind=jnp.bfloat16):
    level = block_levels(key, shape, split, -0.22, 0.18) if split else 1.0
    array = jax.random.normal(key, shape, jnp.float32) * scale * level
    return jnp.minimum(jnp.maximum(array, -reach), reach).astype(kind)


def setup_inputs(seed: int = 0) -> dict:
    keys = jax.random.split(jax.random.key(seed), 11)
    volume = centred(keys[0], (BATCH, DEPTH, HEIGHT, WIDE, C), 1.0, 6.0, ((0, 8), (1, 16), (2, 2)))
    patch_mask = with_ends((jax.random.randint(keys[1], (BATCH, DEPTH, HEIGHT, WIDE), 0, 5) < 3).astype(jnp.int32), jax.random.fold_in(keys[1], 1), 0, 1)
    mask_token = centred(keys[2], (C,), 1.0, 4.0)
    labels = with_ends(jax.random.randint(keys[3], (BATCH, DEPTH, HEIGHT, WIDE), 0, 4), jax.random.fold_in(keys[3], 1), 0, 3).astype(jnp.int32)
    norm_gain = jnp.clip(1.0 + 0.18 * jax.random.normal(keys[4], (C,), jnp.float32), 0.1, 1.9)
    qkv_weight = draw_qkv_weight(jax.random.fold_in(keys[10], 71), 0)
    proj_weight = centred(keys[6], (ATTN, C), ATTN ** -0.5, 0.4375)
    merge_gain = jnp.clip(1.0 + 0.18 * jax.random.normal(keys[7], (8 * C,), jnp.float32), 0.1, 1.9)
    merge_weight = centred(keys[8], (8 * C, 2 * C), (8 * C) ** -0.5, 0.109375, ((1, 2),))
    upstream = centred(keys[9], (BATCH, DEPTH, HEIGHT, WIDE, C), 1.0, 6.0, ((0, 8), (1, 16), (2, 2)))
    return {"volume": volume, "patch_mask": patch_mask, "mask_token": mask_token, "labels": labels, "norm_gain": norm_gain, "qkv_weight": qkv_weight, "proj_weight": proj_weight, "merge_gain": merge_gain, "merge_weight": merge_weight, "upstream": upstream}


def layer_norm(values, gain_vector):
    row_mean = lax.optimization_barrier(jnp.mean(values, axis=-1, keepdims=True))
    centered = values - row_mean
    variance = lax.optimization_barrier(jnp.mean(centered * centered, axis=-1, keepdims=True))
    return centered * lax.rsqrt(variance + 1e-05) * gain_vector

def to_windows(grid, window):
    blocked = grid.reshape(grid.shape[0], grid.shape[1] // window, window, grid.shape[2] // window, window, grid.shape[3] // window, window, grid.shape[4])
    return blocked.transpose(0, 1, 3, 5, 2, 4, 6, 7).reshape(-1, window ** 3, grid.shape[4])

def from_windows(pieces, target, window):
    blocked = pieces.reshape(target[0], target[1] // window, target[2] // window, target[3] // window, window, window, window, target[4])
    return blocked.transpose(0, 1, 4, 2, 5, 3, 6, 7).reshape(target)

def to_cells(grid):
    blocked = grid.reshape(grid.shape[0], grid.shape[1] // 2, 2, grid.shape[2] // 2, 2, grid.shape[3] // 2, 2, grid.shape[4])
    return blocked.transpose(0, 1, 3, 5, 2, 4, 6, 7).reshape(grid.shape[0], grid.shape[1] // 2, grid.shape[2] // 2, grid.shape[3] // 2, 8 * grid.shape[4])

def attend(normed_w, label_w, cot_w, qkv_weight, proj_weight):
    count = normed_w.shape[0]
    head_dim = qkv_weight.shape[1] // (3 * HEADS)
    score_scale = head_dim ** (-0.5)
    projections = jnp.dot(normed_w, qkv_weight, preferred_element_type=jnp.float32).astype(jnp.bfloat16)
    projections = projections.reshape(count, 3, HEADS, head_dim).astype(jnp.float32)
    query_rows = projections[:, 0]
    key_rows = projections[:, 1]
    value_rows = projections[:, 2]
    scores = jnp.einsum('qhd,khd->hqk', query_rows, key_rows) * score_scale
    same_label = label_w[:, None] == label_w[None, :]
    scores = jnp.where(same_label[None], scores, -jnp.inf)
    row_max = lax.optimization_barrier(jnp.max(scores, axis=-1, keepdims=True))
    exponent = jnp.exp(scores - row_max)
    probability = exponent / lax.optimization_barrier(jnp.sum(exponent, axis=-1, keepdims=True))
    weights = probability.astype(jnp.bfloat16).astype(jnp.float32)
    context_full = jnp.einsum('hqk,khd->qhd', weights, value_rows)
    context = context_full.astype(jnp.bfloat16).reshape(count, HEADS * head_dim)
    attended = jnp.dot(context, proj_weight, preferred_element_type=jnp.float32).astype(jnp.bfloat16)
    grad_proj = jnp.dot(context.T, cot_w, preferred_element_type=jnp.float32)
    dcontext = jnp.dot(cot_w, proj_weight.T, preferred_element_type=jnp.float32).astype(jnp.bfloat16)
    dcontext = dcontext.reshape(count, HEADS, head_dim).astype(jnp.float32)
    dweights = jnp.einsum('qhd,khd->hqk', dcontext, value_rows)
    inner = jnp.einsum('qhd,qhd->hq', dcontext, context_full)[..., None]
    dscores = (weights * (dweights - inner) * score_scale).astype(jnp.bfloat16).astype(jnp.float32)
    dquery = jnp.einsum('hqk,khd->qhd', dscores, key_rows)
    dkey = jnp.einsum('hqk,qhd->khd', dscores, query_rows)
    dvalue = jnp.einsum('hqk,qhd->khd', weights, dcontext)
    dprojections = jnp.stack((dquery, dkey, dvalue), 1).astype(jnp.bfloat16).reshape(count, 3 * HEADS * head_dim)
    grad_qkv = jnp.dot(normed_w.T, dprojections, preferred_element_type=jnp.float32)
    return (attended, grad_proj, grad_qkv)

def reference(volume, patch_mask, mask_token, labels, norm_gain, qkv_weight, proj_weight, merge_gain, merge_weight, upstream):
    tokens = jnp.where(patch_mask[..., None] == 1, mask_token, volume)
    offsets = (-SHIFT, -SHIFT, -SHIFT)
    rolled = jnp.roll(tokens, offsets, axis=(1, 2, 3))
    rolled_cot = jnp.roll(upstream, offsets, axis=(1, 2, 3))
    normed = layer_norm(rolled.astype(jnp.float32), norm_gain).astype(jnp.bfloat16)
    normed_w = to_windows(normed, WIN)
    label_w = to_windows(labels[..., None], WIN)[..., 0]
    cot_w = to_windows(rolled_cot, WIN)
    window_count = normed_w.shape[0]
    group_size = 4
    grouped = (normed_w.reshape(window_count // group_size, group_size, WIN ** 3, normed_w.shape[2]), label_w.reshape(window_count // group_size, group_size, WIN ** 3), cot_w.reshape(window_count // group_size, group_size, WIN ** 3, cot_w.shape[2]))

    def advance(totals, inputs):
        attended, grad_proj, grad_qkv = jax.vmap(attend, in_axes=(0, 0, 0, None, None))(inputs[0], inputs[1], inputs[2], qkv_weight, proj_weight)
        return ((totals[0] + lax.optimization_barrier(jnp.sum(grad_qkv, 0)), totals[1] + lax.optimization_barrier(jnp.sum(grad_proj, 0))), attended)
    initial = (jnp.zeros(qkv_weight.shape, jnp.float32), jnp.zeros(proj_weight.shape, jnp.float32))
    (grad_qkv, grad_proj), attended = lax.scan(advance, initial, grouped)
    attended = from_windows(attended.reshape(window_count, WIN ** 3, attended.shape[-1]), tokens.shape, WIN)
    restored = jnp.roll(attended, (SHIFT, SHIFT, SHIFT), axis=(1, 2, 3))
    block_out = (tokens.astype(jnp.float32) + restored.astype(jnp.float32)).astype(jnp.bfloat16)
    features = layer_norm(to_cells(block_out).astype(jnp.float32), merge_gain).astype(jnp.bfloat16)
    merged = jnp.dot(features, merge_weight, preferred_element_type=jnp.float32).astype(jnp.bfloat16)
    return (merged, grad_qkv, grad_proj)
```

```python
import functools
import math

import jax
import jax.numpy as jnp
import numpy as np
from jax import lax
from jax.experimental import pallas as pl
from jax.experimental.pallas import tpu as pltpu
from jax.sharding import PartitionSpec as P

HEADS = 6
HEAD = 32
ATTN = 192
C = 384
WIN = 7
SHIFT = 3
EDGE = 14
PITCH = 16
SLAB = EDGE * PITCH
ROWS = 384
FEED = C + ATTN
EPS = 1e-05
F32 = jnp.float32
BF16 = jnp.bfloat16
MESH = pl.DeviceIdType.MESH
VMEM_LIMIT = 56 * 2**20

SIZES = (3, 7, 4)
FIRST = (0, 3, 10)
ZONES = [(a, b) for a in range(3) for b in range(3)]


def up(value, unit):
    return -(-value // unit) * unit


ZONE_ROWS = {z: up(WIN * SIZES[z[0]] * SIZES[z[1]], 16) for z in ZONES}
ZONE_BASE = {}
TOTAL = 0
for zone in ZONES:
    ZONE_BASE[zone] = TOTAL
    TOTAL += ZONE_ROWS[zone]
PIECE_ROWS = tuple(up(WIN * s, 8) for s in SIZES)
PIECES = []
_at = 0
for _half in range(2):
    for _hz in range(3):
        PIECES.append((_half, _hz, _at))
        _at += PIECE_ROWS[_hz]

GROUPS = {
    (0, 0): ((1, 1),),
    (0, 1): ((1, 2), (1, 0)),
    (1, 0): ((2, 1), (0, 1)),
    (1, 1): ((2, 2), (2, 0), (0, 2), (0, 0)),
}


def slab_to_pieces():
    pick = np.zeros((SLAB, SLAB), np.float32)
    for half, hz, base in PIECES:
        for hh in range(SIZES[hz]):
            for k in range(WIN):
                width = (SHIFT + WIN * half + k) % EDGE
                pick[base + hh * WIN + k, (FIRST[hz] + hh) * PITCH + width] = 1
    return pick


def slab_to_cells():
    pick = np.zeros((SLAB, SLAB), np.float32)
    for hh in range(2):
        for ww in range(2):
            for h in range(7):
                for w in range(7):
                    pick[(hh * 2 + ww) * 56 + h * 8 + w, (2 * h + hh) * PITCH + 2 * w + ww] = 1
    return pick


def nn(a, b):
    return jnp.dot(a, b, preferred_element_type=F32)


def nt(a, b):
    return lax.dot_general(a, b, (((1,), (1,)), ((), ())), preferred_element_type=F32)


def tn(a, b):
    return lax.dot_general(a, b, (((0,), (0,)), ((), ())), preferred_element_type=F32)


def masked_pick(pick, mask_row):
    hidden = pick * mask_row
    return pick - hidden, jnp.sum(hidden.astype(F32), axis=1, keepdims=True)


def prep_kernel(vol, ups, mask, pick, token, gain, proj_t, *rest):
    outs, (space, pad_v, pad_u) = rest[:9], rest[9:]
    space[...] = jnp.zeros_like(space)
    pad_v[...] = jnp.zeros_like(pad_v)
    pad_u[...] = jnp.zeros_like(pad_u)
    for d in range(EDGE):
        dz = 0 if d < FIRST[1] else 1 if d < FIRST[2] else 2
        at = d - FIRST[dz]
        for h in range(EDGE):
            pad_v[d % 2, h, 0:EDGE, :] = vol[0, d, h]
            pad_u[d % 2, h, 0:EDGE, :] = ups[0, d, h]
        shown, hidden = masked_pick(pick[...], mask[d])
        tokens = nn(shown, pad_v[d % 2].reshape(SLAB, C)) + hidden * token[...]
        mean = jnp.mean(tokens, axis=1, keepdims=True)
        centered = tokens - mean
        variance = jnp.mean(centered * centered, axis=1, keepdims=True)
        normed = centered * lax.rsqrt(variance + EPS) * gain[...]
        dcontext = nn(nn(pick[...], pad_u[d % 2].reshape(SLAB, C)).astype(BF16), proj_t[...])
        for half, hz, base in PIECES:
            size = WIN * SIZES[hz]
            row = ZONE_BASE[(dz, hz)] + at * size
            space[half, row : row + size, 0:C] = normed[base : base + size]
            space[half, row : row + size, C:FEED] = dcontext[base : base + size]
    for out, zone in zip(outs, ZONES):
        base = ZONE_BASE[zone]
        out[...] = space[:, base : base + ZONE_ROWS[zone], :].astype(BF16)


def prep(volume, upstream, mask, pick, token, gain, proj_t):
    return pl.pallas_call(
        prep_kernel,
        out_shape=[jax.ShapeDtypeStruct((2, ZONE_ROWS[z], FEED), BF16) for z in ZONES],
        scratch_shapes=[
            pltpu.VMEM((2, TOTAL, FEED), F32),
            pltpu.VMEM((2, EDGE, PITCH, C), BF16),
            pltpu.VMEM((2, EDGE, PITCH, C), BF16),
        ],
        compiler_params=pltpu.CompilerParams(vmem_limit_bytes=VMEM_LIMIT),
        name="prep",
    )(volume, upstream, mask, pick, token, gain, proj_t)


def attend_kernel(zones, has_total, *refs):
    count = len(zones)
    parts, refs = refs[:count], refs[count:]
    label, weight, weight_t, eye = refs[:4]
    refs = refs[4:]
    if has_total:
        total, refs = refs[0], refs[1:]
    outs, refs = refs[:count], refs[count:]
    grad, x, bias, proj, proj_t, dcon_t, con_t, dproj_t = refs
    row = 0
    for part, zone in zip(parts, zones):
        x[row : row + ZONE_ROWS[zone], :] = part[0]
        row += ZONE_ROWS[zone]
    x[row:ROWS, :] = jnp.zeros((ROWS - row, FEED), BF16)
    scale = HEAD**-0.5
    normed = x[:, 0:C]
    label_row = label[0]
    label_column = jnp.transpose(jnp.broadcast_to(label_row, (8, ROWS)))[:, 0:1]
    bias[...] = jnp.where(label_column == label_row, 0.0, -1e30)
    proj[...] = nn(normed, weight[...]).astype(BF16)
    proj_t[...] = nt(weight_t[...], normed).astype(BF16)
    dcon_t[...] = nt(eye[...], x[:, C:FEED]).astype(BF16)
    for head in range(HEADS):
        a, b, c = (slice(i * ATTN + head * HEAD, i * ATTN + head * HEAD + HEAD) for i in range(3))
        scores = nn(proj[:, b], proj_t[a, :]) * (scale * math.log2(math.e)) + bias[...]
        exponent = jnp.exp2(scores - jnp.max(scores, axis=0, keepdims=True))
        weights = (exponent * (1.0 / jnp.sum(exponent, axis=0, keepdims=True))).astype(BF16)
        context_t = nn(proj_t[c, :], weights)
        con_t[a, :] = context_t
        inner = jnp.sum(dcon_t[a, :].astype(F32) * context_t, axis=0, keepdims=True)
        dweights = nn(proj[:, c], dcon_t[a, :])
        dscores = (weights.astype(F32) * (dweights - inner) * scale).astype(BF16)
        dproj_t[a, :] = nn(proj_t[b, :], dscores).astype(BF16)
        dproj_t[b, :] = jnp.transpose(nn(dscores, proj[:, a])).astype(BF16)
        cot = x[:, C + head * HEAD : C + head * HEAD + HEAD]
        dproj_t[c, :] = jnp.transpose(nn(weights, cot)).astype(BF16)
    context = jnp.transpose(con_t[...]).astype(BF16)
    row = 0
    for out, zone in zip(outs, zones):
        out[0] = context[row : row + ZONE_ROWS[zone]]
        row += ZONE_ROWS[zone]
    term = nn(dproj_t[...], normed)
    first = pl.program_id(0) == 0

    @pl.when(first)
    def _():
        grad[...] = term + total[...] if has_total else term

    @pl.when(jnp.logical_not(first))
    def _():
        grad[...] += term


def attend(zones, parts, label, weight, weight_t, eye, total):
    def whole(array):
        return pl.BlockSpec(array.shape, lambda i: (0,) * array.ndim)

    def halves(shape):
        return pl.BlockSpec((1,) + shape, lambda i: (i, 0, 0))

    shared = [weight, weight_t, eye] + ([] if total is None else [total])
    contexts = [(ZONE_ROWS[z], ATTN) for z in zones]
    results = pl.pallas_call(
        functools.partial(attend_kernel, zones, total is not None),
        grid=(2,),
        out_shape=[jax.ShapeDtypeStruct((2,) + s, BF16) for s in contexts]
        + [jax.ShapeDtypeStruct((3 * ATTN, C), F32)],
        in_specs=[halves(p.shape[1:]) for p in parts] + [halves((1, ROWS))] + [whole(s) for s in shared],
        out_specs=[halves(s) for s in contexts] + [pl.BlockSpec((3 * ATTN, C), lambda i: (0, 0))],
        scratch_shapes=[
            pltpu.VMEM((ROWS, FEED), BF16),
            pltpu.VMEM((ROWS, ROWS), F32),
            pltpu.VMEM((ROWS, 3 * ATTN), BF16),
            pltpu.VMEM((3 * ATTN, ROWS), BF16),
            pltpu.VMEM((ATTN, ROWS), BF16),
            pltpu.VMEM((ATTN, ROWS), F32),
            pltpu.VMEM((3 * ATTN, ROWS), BF16),
        ],
        cost_estimate=pl.CostEstimate(flops=20_000_000_000, bytes_accessed=4_000_000, transcendentals=2_000_000),
        compiler_params=pltpu.CompilerParams(vmem_limit_bytes=VMEM_LIMIT),
        name="attend",
    )(*parts, label, *shared)
    return results[:-1], results[-1]


def merge_kernel(vol, ups, mask, pick, back, cells, token, proj, gain, own, other, *rest):
    contexts, rest = rest[:9], rest[9:]
    own_out, other_out, grad_out, space, pad_v, pad_u, context_all, features = rest
    space[:, TOTAL:, :] = jnp.zeros((2, space.shape[1] - TOTAL, ATTN), F32)
    for context, zone in zip(contexts, ZONES):
        base = ZONE_BASE[zone]
        space[:, base : base + ZONE_ROWS[zone], :] = context[...].astype(F32)
    pad_v[...] = jnp.zeros_like(pad_v)
    pad_u[...] = jnp.zeros_like(pad_u)
    for pair in range(EDGE // 2):
        blocks = []
        for d in (2 * pair, 2 * pair + 1):
            dz = 0 if d < FIRST[1] else 1 if d < FIRST[2] else 2
            at = d - FIRST[dz]
            for h in range(EDGE):
                pad_v[d % 2, h, 0:EDGE, :] = vol[0, d, h]
                pad_u[d, h, 0:EDGE, :] = ups[0, d, h]
            pieces = []
            for half, hz, _ in PIECES:
                row = ZONE_BASE[(dz, hz)] + at * WIN * SIZES[hz]
                pieces.append(space[half, row : row + PIECE_ROWS[hz], :])
            context = nn(back[...], jnp.concatenate(pieces, axis=0).astype(BF16)).astype(BF16)
            context_all[d * SLAB : (d + 1) * SLAB, :] = context
            attended = nn(context, proj[...]).astype(BF16)
            shown, hidden = masked_pick(cells[...], mask[d])
            tokens = nn(shown, pad_v[d % 2].reshape(SLAB, C)) + hidden * token[...]
            block = (tokens + nn(cells[...], attended)).astype(BF16).astype(F32)
            blocks += [block[o * 56 : o * 56 + 56] for o in range(4)]
        total = sum(blocks[1:], blocks[0])
        mean = jnp.sum(total, axis=1, keepdims=True) * (1.0 / (8 * C))
        centered = [b - mean for b in blocks]
        squares = [b * b for b in centered]
        variance = jnp.sum(sum(squares[1:], squares[0]), axis=1, keepdims=True) * (1.0 / (8 * C))
        factor = lax.rsqrt(variance + EPS)
        for o in range(8):
            values = (centered[o] * factor * gain[o : o + 1, :]).astype(BF16)
            features[pair * 56 : pair * 56 + 56, o * C : (o + 1) * C] = values.astype(F32)
    merged = features[...].astype(BF16)
    own_out[...] = nn(merged, own[...]).astype(BF16)
    other_out[...] = nn(merged, other[...]).astype(BF16)
    grad_out[...] = tn(context_all[...], pad_u[...].reshape(EDGE * SLAB, C))


def merge(volume, upstream, mask, pick, back, cells, token, proj, gain, own, other, contexts):
    cells_out = jax.ShapeDtypeStruct((7 * 56, C), BF16)
    return pl.pallas_call(
        merge_kernel,
        out_shape=[cells_out, cells_out, jax.ShapeDtypeStruct((ATTN, C), F32)],
        scratch_shapes=[
            pltpu.VMEM((2, TOTAL + 32, ATTN), F32),
            pltpu.VMEM((2, EDGE, PITCH, C), BF16),
            pltpu.VMEM((EDGE, EDGE, PITCH, C), BF16),
            pltpu.VMEM((EDGE * SLAB, ATTN), BF16),
            pltpu.VMEM((7 * 56, 8 * C), F32),
        ],
        compiler_params=pltpu.CompilerParams(vmem_limit_bytes=VMEM_LIMIT),
        name="merge",
    )(volume, upstream, mask, pick, back, cells, token, proj, gain, own, other, *contexts)


def reduce_kernel(sizes, terms, out, arrived, summed, gathered, send_a, recv_a, send_b, recv_b):
    depths, heights, batches = sizes
    owners = depths * heights
    depth, height, batch = (lax.axis_index(n) for n in ("depth", "height", "batch"))
    me = depth * heights + height

    def owner_at(step):
        other = lax.rem(me + step, owners)
        return {"depth": other // heights, "height": lax.rem(other, heights)}

    def batch_at(step):
        return {"batch": lax.rem(batch + step, batches)}

    barrier = pltpu.get_barrier_semaphore()

    @pl.loop(1, owners)
    def _(step):
        pl.semaphore_signal(barrier, inc=1, device_id=owner_at(step), device_id_type=MESH)

    @pl.loop(1, batches)
    def _(step):
        pl.semaphore_signal(barrier, inc=1, device_id=batch_at(step), device_id_type=MESH)

    pl.semaphore_wait(barrier, owners + batches - 2)

    def to_owner(step):
        return pltpu.make_async_remote_copy(
            src_ref=terms.at[lax.rem(me + step, owners)],
            dst_ref=arrived.at[step],
            send_sem=send_a.at[step],
            recv_sem=recv_a.at[step],
            device_id=owner_at(step),
            device_id_type=MESH,
        )

    @pl.loop(1, owners)
    def _(step):
        to_owner(step).start()

    summed[...] = terms[me].astype(F32)

    @pl.loop(1, owners)
    def _(step):
        to_owner(step).wait_recv()
        summed[...] += arrived[step].astype(F32)

    def to_batch(step):
        return pltpu.make_async_remote_copy(
            src_ref=summed,
            dst_ref=gathered.at[step],
            send_sem=send_b.at[step],
            recv_sem=recv_b.at[step],
            device_id=batch_at(step),
            device_id_type=MESH,
        )

    @pl.loop(1, batches)
    def _(step):
        to_batch(step).start()

    out[...] = summed[...]

    @pl.loop(1, batches)
    def _(step):
        to_batch(step).wait_recv()
        out[...] += gathered[step]

    @pl.loop(1, owners)
    def _(step):
        to_owner(step).wait_send()

    @pl.loop(1, batches)
    def _(step):
        to_batch(step).wait_send()


def reduce_terms(terms, sizes):
    owners, (rows, columns) = sizes[0] * sizes[1], terms.shape[1:]
    vmem = pl.BlockSpec(memory_space=pltpu.VMEM)
    return pl.pallas_call(
        functools.partial(reduce_kernel, sizes),
        out_shape=jax.ShapeDtypeStruct((rows, columns), F32),
        in_specs=[vmem],
        out_specs=vmem,
        scratch_shapes=[
            pltpu.VMEM((owners, rows, columns), terms.dtype),
            pltpu.VMEM((rows, columns), F32),
            pltpu.VMEM((sizes[2], rows, columns), F32),
            pltpu.SemaphoreType.DMA((owners,)),
            pltpu.SemaphoreType.DMA((owners,)),
            pltpu.SemaphoreType.DMA((sizes[2],)),
            pltpu.SemaphoreType.DMA((sizes[2],)),
        ],
        compiler_params=pltpu.CompilerParams(
            collective_id=0, has_side_effects=True, vmem_limit_bytes=VMEM_LIMIT
        ),
        name="reduce",
    )(terms)


def shifted(array, axes, by):
    sizes = [lax.axis_size(a) for a in axes]
    pairs = []
    for source in np.ndindex(*sizes):
        target = [(s + by) % n for s, n in zip(source, sizes)]
        pairs.append((int(np.ravel_multi_index(source, sizes)), int(np.ravel_multi_index(target, sizes))))
    return lax.ppermute(array, axes if len(axes) > 1 else axes[0], pairs)


def group_labels(labels, group):
    parts = []
    for zone in GROUPS[group]:
        spans = []
        for z in zone:
            start = {1: 0, 2: WIN, 0: WIN + SIZES[2]}[z]
            spans.append((start, SIZES[z]))
        (d, nd), (h, nh) = spans
        part = labels[d : d + nd, h : h + nh].reshape(nd, nh, 2, WIN).transpose(2, 0, 1, 3)
        part = part.reshape(2, nd * nh * WIN)
        parts.append(jnp.pad(part, ((0, 0), (0, ZONE_ROWS[zone] - nd * nh * WIN)), constant_values=-1))
    row = jnp.concatenate(parts, axis=1)
    row = jnp.pad(row, ((0, 0), (0, ROWS - row.shape[1])), constant_values=-1)
    return row.reshape(2, 1, ROWS).astype(F32)


def shards(
    volume,
    patch_mask,
    mask_token,
    labels,
    norm_gain,
    qkv_weight,
    proj_weight,
    merge_gain,
    merge_weight,
    upstream,
):
    sizes = tuple(lax.axis_size(n) for n in ("depth", "height", "batch"))
    height, batch = lax.axis_index("height"), lax.axis_index("batch")
    pick_np = slab_to_pieces()
    pick = jnp.asarray(pick_np, BF16)
    back = jnp.asarray(pick_np.T, BF16)
    cells = jnp.asarray(slab_to_cells(), BF16)
    eye = jnp.asarray(np.eye(ATTN), BF16)
    token = mask_token.reshape(1, C).astype(F32)
    mask = jnp.pad(patch_mask[0], ((0, 0), (0, 0), (0, PITCH - EDGE))).reshape(EDGE, 1, SLAB).astype(BF16)
    made = prep(volume, upstream, mask, pick, token, norm_gain.reshape(1, C), proj_weight.T)
    zone = dict(zip(ZONES, made))
    by_height = shifted(jnp.concatenate((zone[1, 0], zone[2, 0]), 1), ("height",), -1)
    by_depth = shifted(jnp.concatenate((zone[0, 1], zone[0, 2]), 1), ("depth",), -1)
    by_both = shifted(zone[0, 0], ("depth", "height"), -1)

    label = {group: group_labels(labels[0], group) for group in GROUPS}
    shared = (qkv_weight, qkv_weight.T, eye)

    def run(group, parts, total):
        return attend(GROUPS[group], parts, label[group], *shared, total)

    context = {}
    (context[1, 1],), total = run((0, 0), [zone[1, 1]], None)
    split = ZONE_ROWS[1, 0]
    (context[1, 2], back_h), total = run((0, 1), [zone[1, 2], by_height[:, :split]], total)
    context[1, 0] = shifted(back_h, ("height",), 1)
    (context[2, 1], back_d), total = run((1, 0), [zone[2, 1], by_depth[:, :split]], total)
    context[0, 1] = shifted(back_d, ("depth",), 1)
    (context[2, 2], back_h, back_d, back_b), total = run(
        (1, 1), [zone[2, 2], by_height[:, split:], by_depth[:, split:], by_both], total
    )
    context[2, 0] = shifted(back_h, ("height",), 1)
    context[0, 2] = shifted(back_d, ("depth",), 1)
    context[0, 0] = shifted(back_b, ("depth", "height"), 1)

    share = 8 * C // sizes[2]
    rows = lax.dynamic_slice_in_dim(merge_weight, batch * share, share, 0)
    rows, _ = lax.optimization_barrier((rows, by_height))
    other = lax.all_gather(shifted(rows, ("height",), 1), "batch", axis=0, tiled=True)

    own_part, other_part, grad_proj = merge(
        volume,
        upstream,
        mask,
        pick,
        back,
        cells,
        token,
        proj_weight,
        merge_gain.reshape(8, C),
        merge_weight,
        other,
        [context[z] for z in ZONES],
    )
    fetched = shifted(other_part, ("height",), 1)
    owners = sizes[0] * sizes[1]
    terms = jnp.concatenate(
        (total.T.reshape(owners, -1, 3 * ATTN), grad_proj.reshape(owners, -1, 3 * ATTN)), 1
    ).astype(BF16)
    sums = reduce_terms(terms, sizes)
    lines = C // owners
    grad_qkv = sums[:lines]
    grad_proj = sums[lines:].reshape(ATTN // owners, C)

    halves = [part.reshape(7, 7, 8, C)[:, :, :7] for part in (own_part, fetched)]
    low = jnp.where(height == 0, halves[0], halves[1])
    high = jnp.where(height == 0, halves[1], halves[0])
    merged = jnp.concatenate((low, high), 1)[None]
    return (merged, grad_qkv, grad_proj)


def solution(mesh):
    return jax.shard_map(
        shards,
        mesh=mesh,
        in_specs=(
            P("batch", "depth", "height", None, None),
            P("batch", "depth", "height", None),
            P(),
            P("batch", "depth", "height", None),
            P(),
            P(),
            P(),
            P(),
            P(None, "height"),
            P("batch", "depth", "height", None, None),
        ),
        out_specs=(
            P("batch", "depth", None, None, "height"),
            P(("depth", "height"), None),
            P(("depth", "height"), None),
        ),
        check_vma=False,
    )
```

```python
import functools
import math

import jax
import jax.numpy as jnp
import numpy as np
from jax import lax
from jax.experimental import pallas as pl
from jax.experimental.pallas import tpu as pltpu
from jax.sharding import PartitionSpec as P

HEADS = 6
HEAD = 32
ATTN = 192
C = 384
WIN = 7
SHIFT = 3
EDGE = 14
PITCH = 16
SLAB = EDGE * PITCH
ROWS = 384
FEED = C + ATTN
EPS = 1e-05
F32 = jnp.float32
BF16 = jnp.bfloat16
MESH = pl.DeviceIdType.MESH
VMEM_LIMIT = 56 * 2**20

SIZES = (3, 7, 4)
FIRST = (0, 3, 10)
ZONES = [(a, b) for a in range(3) for b in range(3)]


def up(value, unit):
    return -(-value // unit) * unit


ZONE_ROWS = {z: up(WIN * SIZES[z[0]] * SIZES[z[1]], 16) for z in ZONES}
ZONE_BASE = {}
TOTAL = 0
for zone in ZONES:
    ZONE_BASE[zone] = TOTAL
    TOTAL += ZONE_ROWS[zone]
PIECE_ROWS = tuple(up(WIN * s, 8) for s in SIZES)
PIECES = []
_at = 0
for _half in range(2):
    for _hz in range(3):
        PIECES.append((_half, _hz, _at))
        _at += PIECE_ROWS[_hz]

GROUPS = {
    (0, 0): ((1, 1),),
    (0, 1): ((1, 2), (1, 0)),
    (1, 0): ((2, 1), (0, 1)),
    (1, 1): ((2, 2), (2, 0), (0, 2), (0, 0)),
}


def slab_to_pieces():
    pick = np.zeros((SLAB, SLAB), np.float32)
    for half, hz, base in PIECES:
        for hh in range(SIZES[hz]):
            for k in range(WIN):
                width = (SHIFT + WIN * half + k) % EDGE
                pick[base + hh * WIN + k, (FIRST[hz] + hh) * PITCH + width] = 1
    return pick


def slab_to_cells():
    pick = np.zeros((SLAB, SLAB), np.float32)
    for hh in range(2):
        for ww in range(2):
            for h in range(7):
                for w in range(7):
                    pick[(hh * 2 + ww) * 56 + h * 8 + w, (2 * h + hh) * PITCH + 2 * w + ww] = 1
    return pick


def nn(a, b):
    return jnp.dot(a, b, preferred_element_type=F32)


def nt(a, b):
    return lax.dot_general(a, b, (((1,), (1,)), ((), ())), preferred_element_type=F32)


def tn(a, b):
    return lax.dot_general(a, b, (((0,), (0,)), ((), ())), preferred_element_type=F32)


def masked_pick(pick, mask_row):
    hidden = pick * mask_row
    return pick - hidden, jnp.sum(hidden.astype(F32), axis=1, keepdims=True)


AHEAD = {}
for _group, _members in GROUPS.items():
    _row = 0
    for zone in _members:
        if 0 in zone:
            AHEAD[zone] = (_group, _row)
        _row += ZONE_ROWS[zone]
HALO = list(AHEAD)
GROUP_LIST = list(GROUPS)


def neighbour(zone, by, sizes):
    device = {}
    for axis, part, size in zip(("depth", "height"), zone, sizes):
        if part == 0:
            device[axis] = lax.rem(lax.axis_index(axis) + by + size, size)
    return device


def front_kernel(sizes, vol, ups, mask, label, pick, token, gain, back_proj, weight, weight_t, eye, *rest):
    context_out, grad, x, space, pad_v, pad_u = rest[:6]
    send_buffers, rest = dict(zip(HALO, rest[6:11])), rest[11:]
    context_w, context_z, bias, proj, proj_t, dcon_t, con_t, dproj_t = rest[:8]
    ahead_send, ahead_recv, back_send, back_recv = rest[8:]

    def ahead(zone):
        group, row = AHEAD[zone]
        slot = HALO.index(zone)
        return pltpu.make_async_remote_copy(
            src_ref=send_buffers[zone],
            dst_ref=x.at[pl.ds(2 * GROUP_LIST.index(group), 2), pl.ds(row, ZONE_ROWS[zone]), :],
            send_sem=ahead_send.at[slot],
            recv_sem=ahead_recv.at[slot],
            device_id=neighbour(zone, -1, sizes),
            device_id_type=MESH,
        )

    def back(zone, half):
        group, row = AHEAD[zone]
        slot = 2 * HALO.index(zone) + half
        return pltpu.make_async_remote_copy(
            src_ref=context_w.at[2 * GROUP_LIST.index(group) + half, pl.ds(row, ZONE_ROWS[zone]), :],
            dst_ref=context_z.at[half, pl.ds(ZONE_BASE[zone], ZONE_ROWS[zone]), :],
            send_sem=back_send.at[slot],
            recv_sem=back_recv.at[slot],
            device_id=neighbour(zone, 1, sizes),
            device_id_type=MESH,
        )

    barrier = pltpu.get_barrier_semaphore()
    met = [((0, 1), -1), ((0, 1), 1), ((1, 0), 1), ((0, 0), -1), ((0, 0), 1)]
    for zone, by in met:
        pl.semaphore_signal(barrier, inc=1, device_id=neighbour(zone, by, sizes), device_id_type=MESH)

    space[...] = jnp.zeros_like(space)
    pad_v[...] = jnp.zeros_like(pad_v)
    pad_u[...] = jnp.zeros_like(pad_u)
    for number, group in enumerate(GROUP_LIST):
        used = sum(ZONE_ROWS[zone] for zone in GROUPS[group])
        x[2 * number : 2 * number + 2, used:, :] = jnp.zeros((2, ROWS - used, FEED), BF16)
    for d in range(EDGE):
        dz = 0 if d < FIRST[1] else 1 if d < FIRST[2] else 2
        at = d - FIRST[dz]
        for h in range(EDGE):
            pad_v[d % 2, h, 0:EDGE, :] = vol[0, d, h]
            pad_u[d % 2, h, 0:EDGE, :] = ups[0, d, h]
        shown, hidden = masked_pick(pick[...], mask[d])
        tokens = nn(shown, pad_v[d % 2].reshape(SLAB, C)) + hidden * token[...]
        mean = jnp.mean(tokens, axis=1, keepdims=True)
        centered = tokens - mean
        variance = jnp.mean(centered * centered, axis=1, keepdims=True)
        normed = centered * lax.rsqrt(variance + EPS) * gain[...]
        dcontext = nn(nn(pick[...], pad_u[d % 2].reshape(SLAB, C)).astype(BF16), back_proj[...])
        for half, hz, base in PIECES:
            size = WIN * SIZES[hz]
            row = ZONE_BASE[(dz, hz)] + at * size
            space[half, row : row + size, 0:C] = normed[base : base + size]
            space[half, row : row + size, C:FEED] = dcontext[base : base + size]
        if at == SIZES[dz] - 1:
            if dz == 0:
                pl.semaphore_wait(barrier, len(met))
            for hz in range(3):
                zone = (dz, hz)
                base, rows = ZONE_BASE[zone], ZONE_ROWS[zone]
                filled = space[:, base : base + rows, :].astype(BF16)
                if zone in AHEAD:
                    send_buffers[zone][...] = filled
                    ahead(zone).start()
                else:
                    group = GROUP_LIST.index(((dz - 1), (hz - 1)))
                    x[2 * group : 2 * group + 2, 0:rows, :] = filled

    grad[...] = jnp.zeros_like(grad)
    scale = HEAD**-0.5

    @pl.loop(0, 8)
    def _(i):
        for number, group in enumerate(GROUP_LIST):
            if number:

                @pl.when(i == 2 * number)
                def _():
                    for zone in GROUPS[group]:
                        if zone in AHEAD:
                            ahead(zone).wait_recv()

        normed = x[i, :, 0:C]
        label_row = label[i]
        label_column = jnp.transpose(jnp.broadcast_to(label_row, (8, ROWS)))[:, 0:1]
        bias[...] = jnp.where(label_column == label_row, 0.0, -1e30)
        proj[...] = nn(normed, weight[...]).astype(BF16)
        proj_t[...] = nt(weight_t[...], normed).astype(BF16)
        dcon_t[...] = nt(eye[...], x[i, :, C:FEED]).astype(BF16)
        for head in range(HEADS):
            a, b, c = (slice(k * ATTN + head * HEAD, k * ATTN + head * HEAD + HEAD) for k in range(3))
            scores = nn(proj[:, b], proj_t[a, :]) * (scale * math.log2(math.e)) + bias[...]
            exponent = jnp.exp2(scores - jnp.max(scores, axis=0, keepdims=True))
            weights = (exponent * (1.0 / jnp.sum(exponent, axis=0, keepdims=True))).astype(BF16)
            context_t = nn(proj_t[c, :], weights)
            con_t[a, :] = context_t
            inner = jnp.sum(dcon_t[a, :].astype(F32) * context_t, axis=0, keepdims=True)
            dweights = nn(proj[:, c], dcon_t[a, :])
            dscores = (weights.astype(F32) * (dweights - inner) * scale).astype(BF16)
            dproj_t[a, :] = nn(proj_t[b, :], dscores).astype(BF16)
            dproj_t[b, :] = jnp.transpose(nn(dscores, proj[:, a])).astype(BF16)
            cot = x[i, :, C + head * HEAD : C + head * HEAD + HEAD]
            dproj_t[c, :] = jnp.transpose(nn(weights, cot)).astype(BF16)
        context_w[i] = jnp.transpose(con_t[...]).astype(BF16)
        grad[...] += nn(dproj_t[...], normed)
        for number, group in enumerate(GROUP_LIST):
            if number:
                for half in range(2):

                    @pl.when(i == 2 * number + half)
                    def _():
                        for zone in GROUPS[group]:
                            if zone in AHEAD:
                                back(zone, half).start()

    for zone in HALO:
        ahead(zone).wait_send()
    for zone in ZONES:
        if zone not in AHEAD:
            group = GROUP_LIST.index((zone[0] - 1, zone[1] - 1))
            base, rows = ZONE_BASE[zone], ZONE_ROWS[zone]
            context_z[:, base : base + rows, :] = context_w[2 * group : 2 * group + 2, 0:rows, :]
    for zone in HALO:
        for half in range(2):
            back(zone, half).wait_recv()
    context_out[...] = context_z[...]
    for zone in HALO:
        for half in range(2):
            back(zone, half).wait_send()


def front(volume, upstream, mask, label, pick, token, gain, back_proj, weight, weight_t, eye, sizes):
    vmem = pl.BlockSpec(memory_space=pltpu.VMEM)
    operands = (volume, upstream, mask, label, pick, token, gain, back_proj, weight, weight_t, eye)
    return pl.pallas_call(
        functools.partial(front_kernel, sizes),
        out_shape=[
            jax.ShapeDtypeStruct((2, TOTAL, ATTN), BF16),
            jax.ShapeDtypeStruct((3 * ATTN, C), F32),
        ],
        in_specs=[vmem] * len(operands),
        out_specs=[vmem] * 2,
        scratch_shapes=[
            pltpu.VMEM((8, ROWS, FEED), BF16),
            pltpu.VMEM((2, TOTAL, FEED), F32),
            pltpu.VMEM((2, EDGE, PITCH, C), BF16),
            pltpu.VMEM((2, EDGE, PITCH, C), BF16),
        ]
        + [pltpu.VMEM((2, ZONE_ROWS[zone], FEED), BF16) for zone in HALO]
        + [
            pltpu.VMEM((8, ROWS, ATTN), BF16),
            pltpu.VMEM((2, TOTAL, ATTN), BF16),
            pltpu.VMEM((ROWS, ROWS), F32),
            pltpu.VMEM((ROWS, 3 * ATTN), BF16),
            pltpu.VMEM((3 * ATTN, ROWS), BF16),
            pltpu.VMEM((ATTN, ROWS), BF16),
            pltpu.VMEM((ATTN, ROWS), F32),
            pltpu.VMEM((3 * ATTN, ROWS), BF16),
            pltpu.SemaphoreType.DMA((5,)),
            pltpu.SemaphoreType.DMA((5,)),
            pltpu.SemaphoreType.DMA((10,)),
            pltpu.SemaphoreType.DMA((10,)),
        ],
        cost_estimate=pl.CostEstimate(flops=60_000_000_000, bytes_accessed=8_000_000, transcendentals=8_000_000),
        compiler_params=pltpu.CompilerParams(
            collective_id=1, has_side_effects=True, vmem_limit_bytes=VMEM_LIMIT
        ),
        name="front",
    )(*operands)


def merge_kernel(vol, ups, mask, pick, back, cells, token, proj, gain, own, other, *rest):
    contexts, own_out, other_out, grad_out, space, pad_v, pad_u, context_all, features = rest
    space[:, TOTAL:, :] = jnp.zeros((2, space.shape[1] - TOTAL, ATTN), F32)
    space[:, 0:TOTAL, :] = contexts[...].astype(F32)
    pad_v[...] = jnp.zeros_like(pad_v)
    pad_u[...] = jnp.zeros_like(pad_u)
    for pair in range(EDGE // 2):
        blocks = []
        for d in (2 * pair, 2 * pair + 1):
            dz = 0 if d < FIRST[1] else 1 if d < FIRST[2] else 2
            at = d - FIRST[dz]
            for h in range(EDGE):
                pad_v[d % 2, h, 0:EDGE, :] = vol[0, d, h]
                pad_u[d, h, 0:EDGE, :] = ups[0, d, h]
            pieces = []
            for half, hz, _ in PIECES:
                row = ZONE_BASE[(dz, hz)] + at * WIN * SIZES[hz]
                pieces.append(space[half, row : row + PIECE_ROWS[hz], :])
            context = nn(back[...], jnp.concatenate(pieces, axis=0).astype(BF16)).astype(BF16)
            context_all[d * SLAB : (d + 1) * SLAB, :] = context
            attended = nn(context, proj[...]).astype(BF16)
            shown, hidden = masked_pick(cells[...], mask[d])
            tokens = nn(shown, pad_v[d % 2].reshape(SLAB, C)) + hidden * token[...]
            block = (tokens + nn(cells[...], attended)).astype(BF16).astype(F32)
            blocks += [block[o * 56 : o * 56 + 56] for o in range(4)]
        total = sum(blocks[1:], blocks[0])
        mean = jnp.sum(total, axis=1, keepdims=True) * (1.0 / (8 * C))
        centered = [b - mean for b in blocks]
        squares = [b * b for b in centered]
        variance = jnp.sum(sum(squares[1:], squares[0]), axis=1, keepdims=True) * (1.0 / (8 * C))
        factor = lax.rsqrt(variance + EPS)
        for o in range(8):
            values = (centered[o] * factor * gain[o : o + 1, :]).astype(BF16)
            features[pair * 56 : pair * 56 + 56, o * C : (o + 1) * C] = values.astype(F32)
    merged = features[...].astype(BF16)
    own_out[...] = nn(merged, own[...]).astype(BF16)
    other_out[...] = nn(merged, other[...]).astype(BF16)
    grad_out[...] = tn(context_all[...], pad_u[...].reshape(EDGE * SLAB, C))


def merge(volume, upstream, mask, pick, back, cells, token, proj, gain, own, other, contexts):
    cells_out = jax.ShapeDtypeStruct((7 * 56, C), BF16)
    return pl.pallas_call(
        merge_kernel,
        out_shape=[cells_out, cells_out, jax.ShapeDtypeStruct((ATTN, C), F32)],
        scratch_shapes=[
            pltpu.VMEM((2, TOTAL + 32, ATTN), F32),
            pltpu.VMEM((2, EDGE, PITCH, C), BF16),
            pltpu.VMEM((EDGE, EDGE, PITCH, C), BF16),
            pltpu.VMEM((EDGE * SLAB, ATTN), BF16),
            pltpu.VMEM((7 * 56, 8 * C), F32),
        ],
        compiler_params=pltpu.CompilerParams(vmem_limit_bytes=VMEM_LIMIT),
        name="merge",
    )(volume, upstream, mask, pick, back, cells, token, proj, gain, own, other, contexts)


def reduce_kernel(sizes, terms, out, arrived, summed, gathered, send_a, recv_a, send_b, recv_b):
    depths, heights, batches = sizes
    owners = depths * heights
    depth, height, batch = (lax.axis_index(n) for n in ("depth", "height", "batch"))
    me = depth * heights + height

    def owner_at(step):
        other = lax.rem(me + step, owners)
        return {"depth": other // heights, "height": lax.rem(other, heights)}

    def batch_at(step):
        return {"batch": lax.rem(batch + step, batches)}

    barrier = pltpu.get_barrier_semaphore()

    @pl.loop(1, owners)
    def _(step):
        pl.semaphore_signal(barrier, inc=1, device_id=owner_at(step), device_id_type=MESH)

    @pl.loop(1, batches)
    def _(step):
        pl.semaphore_signal(barrier, inc=1, device_id=batch_at(step), device_id_type=MESH)

    pl.semaphore_wait(barrier, owners + batches - 2)

    def to_owner(step):
        return pltpu.make_async_remote_copy(
            src_ref=terms.at[lax.rem(me + step, owners)],
            dst_ref=arrived.at[step],
            send_sem=send_a.at[step],
            recv_sem=recv_a.at[step],
            device_id=owner_at(step),
            device_id_type=MESH,
        )

    @pl.loop(1, owners)
    def _(step):
        to_owner(step).start()

    summed[...] = terms[me].astype(F32)

    @pl.loop(1, owners)
    def _(step):
        to_owner(step).wait_recv()
        summed[...] += arrived[step].astype(F32)

    def to_batch(step):
        return pltpu.make_async_remote_copy(
            src_ref=summed,
            dst_ref=gathered.at[step],
            send_sem=send_b.at[step],
            recv_sem=recv_b.at[step],
            device_id=batch_at(step),
            device_id_type=MESH,
        )

    @pl.loop(1, batches)
    def _(step):
        to_batch(step).start()

    out[...] = summed[...]

    @pl.loop(1, batches)
    def _(step):
        to_batch(step).wait_recv()
        out[...] += gathered[step]

    @pl.loop(1, owners)
    def _(step):
        to_owner(step).wait_send()

    @pl.loop(1, batches)
    def _(step):
        to_batch(step).wait_send()


def reduce_terms(terms, sizes):
    owners, (rows, columns) = sizes[0] * sizes[1], terms.shape[1:]
    vmem = pl.BlockSpec(memory_space=pltpu.VMEM)
    return pl.pallas_call(
        functools.partial(reduce_kernel, sizes),
        out_shape=jax.ShapeDtypeStruct((rows, columns), F32),
        in_specs=[vmem],
        out_specs=vmem,
        scratch_shapes=[
            pltpu.VMEM((owners, rows, columns), terms.dtype),
            pltpu.VMEM((rows, columns), F32),
            pltpu.VMEM((sizes[2], rows, columns), F32),
            pltpu.SemaphoreType.DMA((owners,)),
            pltpu.SemaphoreType.DMA((owners,)),
            pltpu.SemaphoreType.DMA((sizes[2],)),
            pltpu.SemaphoreType.DMA((sizes[2],)),
        ],
        compiler_params=pltpu.CompilerParams(
            collective_id=0, has_side_effects=True, vmem_limit_bytes=VMEM_LIMIT
        ),
        name="reduce",
    )(terms)


def shifted(array, axes, by):
    sizes = [lax.axis_size(a) for a in axes]
    pairs = []
    for source in np.ndindex(*sizes):
        target = [(s + by) % n for s, n in zip(source, sizes)]
        pairs.append((int(np.ravel_multi_index(source, sizes)), int(np.ravel_multi_index(target, sizes))))
    return lax.ppermute(array, axes if len(axes) > 1 else axes[0], pairs)


def group_labels(labels, group):
    parts = []
    for zone in GROUPS[group]:
        spans = []
        for z in zone:
            start = {1: 0, 2: WIN, 0: WIN + SIZES[2]}[z]
            spans.append((start, SIZES[z]))
        (d, nd), (h, nh) = spans
        part = labels[d : d + nd, h : h + nh].reshape(nd, nh, 2, WIN).transpose(2, 0, 1, 3)
        part = part.reshape(2, nd * nh * WIN)
        parts.append(jnp.pad(part, ((0, 0), (0, ZONE_ROWS[zone] - nd * nh * WIN)), constant_values=-1))
    row = jnp.concatenate(parts, axis=1)
    row = jnp.pad(row, ((0, 0), (0, ROWS - row.shape[1])), constant_values=-1)
    return row.reshape(2, 1, ROWS).astype(F32)


def shards(
    volume,
    patch_mask,
    mask_token,
    labels,
    norm_gain,
    qkv_weight,
    proj_weight,
    merge_gain,
    merge_weight,
    upstream,
):
    sizes = tuple(lax.axis_size(n) for n in ("depth", "height", "batch"))
    height, batch = lax.axis_index("height"), lax.axis_index("batch")
    pick_np = slab_to_pieces()
    pick = jnp.asarray(pick_np, BF16)
    back = jnp.asarray(pick_np.T, BF16)
    cells = jnp.asarray(slab_to_cells(), BF16)
    eye = jnp.asarray(np.eye(ATTN), BF16)
    token = mask_token.reshape(1, C).astype(F32)
    mask = jnp.pad(patch_mask[0], ((0, 0), (0, 0), (0, PITCH - EDGE))).reshape(EDGE, 1, SLAB).astype(BF16)
    label = jnp.concatenate([group_labels(labels[0], group) for group in GROUP_LIST], 0)
    contexts, total = front(
        volume,
        upstream,
        mask,
        label,
        pick,
        token,
        norm_gain.reshape(1, C),
        proj_weight.T,
        qkv_weight,
        qkv_weight.T,
        eye,
        sizes,
    )

    share = 8 * C // sizes[2]
    rows = lax.dynamic_slice_in_dim(merge_weight, batch * share, share, 0)
    other = lax.all_gather(shifted(rows, ("height",), 1), "batch", axis=0, tiled=True)

    own_part, other_part, grad_proj = merge(
        volume,
        upstream,
        mask,
        pick,
        back,
        cells,
        token,
        proj_weight,
        merge_gain.reshape(8, C),
        merge_weight,
        other,
        contexts,
    )
    fetched = shifted(other_part, ("height",), 1)
    owners = sizes[0] * sizes[1]
    terms = jnp.concatenate(
        (total.T.reshape(owners, -1, 3 * ATTN), grad_proj.reshape(owners, -1, 3 * ATTN)), 1
    ).astype(BF16)
    sums = reduce_terms(terms, sizes)
    lines = C // owners
    grad_qkv = sums[:lines]
    grad_proj = sums[lines:].reshape(ATTN // owners, C)

    halves = [part.reshape(7, 7, 8, C)[:, :, :7] for part in (own_part, fetched)]
    low = jnp.where(height == 0, halves[0], halves[1])
    high = jnp.where(height == 0, halves[1], halves[0])
    merged = jnp.concatenate((low, high), 1)[None]
    return (merged, grad_qkv, grad_proj)


def solution(mesh):
    return jax.shard_map(
        shards,
        mesh=mesh,
        in_specs=(
            P("batch", "depth", "height", None, None),
            P("batch", "depth", "height", None),
            P(),
            P("batch", "depth", "height", None),
            P(),
            P(),
            P(),
            P(),
            P(None, "height"),
            P("batch", "depth", "height", None, None),
        ),
        out_specs=(
            P("batch", "depth", None, None, "height"),
            P(("depth", "height"), None),
            P(("depth", "height"), None),
        ),
        check_vma=False,
    )
```

```python
import functools
import math

import jax
import jax.numpy as jnp
import numpy as np
from jax import lax
from jax.experimental import pallas as pl
from jax.experimental.pallas import tpu as pltpu
from jax.sharding import PartitionSpec as P

HEADS = 6
HEAD = 32
ATTN = 192
C = 384
WIN = 7
SHIFT = 3
EDGE = 14
PITCH = 16
SLAB = EDGE * PITCH
ROWS = 384
FEED = C + ATTN
EPS = 1e-05
F32 = jnp.float32
BF16 = jnp.bfloat16
MESH = pl.DeviceIdType.MESH
VMEM_LIMIT = 56 * 2**20

SIZES = (3, 7, 4)
FIRST = (0, 3, 10)
ZONES = [(a, b) for a in range(3) for b in range(3)]


def up(value, unit):
    return -(-value // unit) * unit


ZONE_ROWS = {z: up(WIN * SIZES[z[0]] * SIZES[z[1]], 16) for z in ZONES}
ZONE_BASE = {}
TOTAL = 0
for zone in ZONES:
    ZONE_BASE[zone] = TOTAL
    TOTAL += ZONE_ROWS[zone]
PIECE_ROWS = tuple(up(WIN * s, 8) for s in SIZES)
PIECES = []
_at = 0
for _half in range(2):
    for _hz in range(3):
        PIECES.append((_half, _hz, _at))
        _at += PIECE_ROWS[_hz]

GROUPS = {
    (0, 0): ((1, 1),),
    (0, 1): ((1, 2), (1, 0)),
    (1, 0): ((2, 1), (0, 1)),
    (1, 1): ((2, 2), (2, 0), (0, 2), (0, 0)),
}


def slab_to_pieces():
    pick = np.zeros((SLAB, SLAB), np.float32)
    for half, hz, base in PIECES:
        for hh in range(SIZES[hz]):
            for k in range(WIN):
                width = (SHIFT + WIN * half + k) % EDGE
                pick[base + hh * WIN + k, (FIRST[hz] + hh) * PITCH + width] = 1
    return pick


def slab_to_cells():
    pick = np.zeros((SLAB, SLAB), np.float32)
    for hh in range(2):
        for ww in range(2):
            for h in range(7):
                for w in range(7):
                    pick[(hh * 2 + ww) * 56 + h * 8 + w, (2 * h + hh) * PITCH + 2 * w + ww] = 1
    return pick


def nn(a, b):
    return jnp.dot(a, b, preferred_element_type=F32)


def nt(a, b):
    return lax.dot_general(a, b, (((1,), (1,)), ((), ())), preferred_element_type=F32)


def tn(a, b):
    return lax.dot_general(a, b, (((0,), (0,)), ((), ())), preferred_element_type=F32)


def masked_pick(pick, mask_row):
    hidden = pick * mask_row
    return pick - hidden, jnp.sum(hidden.astype(F32), axis=1, keepdims=True)


AHEAD = {}
for _group, _members in GROUPS.items():
    _row = 0
    for zone in _members:
        if 0 in zone:
            AHEAD[zone] = (_group, _row)
        _row += ZONE_ROWS[zone]
HALO = list(AHEAD)
GROUP_LIST = list(GROUPS)


def neighbour(zone, by, sizes):
    device = {}
    for axis, part, size in zip(("depth", "height"), zone, sizes):
        if part == 0:
            device[axis] = lax.rem(lax.axis_index(axis) + by + size, size)
    return device


def zone_of(d):
    dz = 0 if d < FIRST[1] else 1 if d < FIRST[2] else 2
    return dz, d - FIRST[dz]


def block_kernel(sizes, *refs):
    depths, heights, batches = sizes
    owners = depths * heights
    lines = C // owners
    vol, ups, mask, label, pick, back_pick, cells, params, weight, weight_p, eye, own = refs[:12]
    merged_out, grad_qkv_out, grad_proj_out = refs[12:15]
    x, space, pad_v, pad_u, context_w, context_z, bias, proj, proj_t, dcon_t, con_t, dproj_t = refs[15:27]
    weight_t, grad, context_space, context_all, features, other, sent, fetched = refs[27:35]
    terms, arrived, total, gathered, ahead_send, ahead_recv, back_send, back_recv = refs[35:43]
    share_send, share_recv, merged_send, merged_recv = refs[43:47]
    term_send, term_recv, sum_send, sum_recv = refs[47:51]
    send_buffers = dict(zip(HALO, refs[51:56]))

    depth, height, batch = (lax.axis_index(n) for n in ("depth", "height", "batch"))
    me = depth * heights + height
    peer = {"height": heights - 1 - height}

    def owner_at(step):
        to = lax.rem(me + step, owners)
        return {"depth": to // heights, "height": lax.rem(to, heights)}

    def batch_at(step):
        return {"batch": lax.rem(batch + step, batches)}

    def remote(src, dst, send, recv, device):
        return pltpu.make_async_remote_copy(
            src_ref=src, dst_ref=dst, send_sem=send, recv_sem=recv, device_id=device, device_id_type=MESH
        )

    def ahead(zone):
        group, row = AHEAD[zone]
        slot = HALO.index(zone)
        landing = x.at[pl.ds(2 * GROUP_LIST.index(group), 2), pl.ds(row, ZONE_ROWS[zone]), :]
        return remote(
            send_buffers[zone], landing, ahead_send.at[slot], ahead_recv.at[slot], neighbour(zone, -1, sizes)
        )

    def back(zone, half):
        group, row = AHEAD[zone]
        slot = 2 * HALO.index(zone) + half
        return remote(
            context_w.at[2 * GROUP_LIST.index(group) + half, pl.ds(row, ZONE_ROWS[zone]), :],
            context_z.at[half, pl.ds(ZONE_BASE[zone], ZONE_ROWS[zone]), :],
            back_send.at[slot],
            back_recv.at[slot],
            neighbour(zone, 1, sizes),
        )

    def first_share():
        return remote(own.at[batch], other.at[0], share_send.at[0], share_recv.at[0], peer)

    def next_share(step):
        return remote(other.at[0], other.at[step], share_send.at[step], share_recv.at[step], batch_at(step))

    def swap_merged():
        return remote(sent, fetched, merged_send.at[0], merged_recv.at[0], peer)

    def term(kind, step):
        return remote(
            terms[kind].at[lax.rem(me + step, owners)],
            arrived[kind].at[step],
            term_send.at[kind, step],
            term_recv.at[kind, step],
            owner_at(step),
        )

    def to_batch(step):
        return remote(total, gathered.at[step], sum_send.at[step], sum_recv.at[step], batch_at(step))

    barrier = pltpu.get_barrier_semaphore()

    @pl.loop(1, owners)
    def _(step):
        pl.semaphore_signal(barrier, inc=1, device_id=owner_at(step), device_id_type=MESH)

    @pl.loop(1, batches)
    def _(step):
        pl.semaphore_signal(barrier, inc=1, device_id=batch_at(step), device_id_type=MESH)

    gain, token = params[0:1, :], params[1:2, :]
    space[...] = jnp.zeros_like(space)
    pad_v[...] = jnp.zeros_like(pad_v)
    pad_u[...] = jnp.zeros_like(pad_u)
    for number, group in enumerate(GROUP_LIST):
        used = sum(ZONE_ROWS[zone] for zone in GROUPS[group])
        x[2 * number : 2 * number + 2, used:, :] = jnp.zeros((2, ROWS - used, FEED), BF16)
    for d in range(EDGE):
        dz, at = zone_of(d)
        for h in range(EDGE):
            pad_v[d % 2, h, 0:EDGE, :] = vol[0, d, h]
            pad_u[d, h, 0:EDGE, :] = ups[0, d, h]
        shown, hidden = masked_pick(pick[...], mask[d])
        tokens = nn(shown, pad_v[d % 2].reshape(SLAB, C)) + hidden * token
        mean = jnp.mean(tokens, axis=1, keepdims=True)
        centered = tokens - mean
        variance = jnp.mean(centered * centered, axis=1, keepdims=True)
        normed = centered * lax.rsqrt(variance + EPS) * gain
        dcontext = nt(nn(pick[...], pad_u[d].reshape(SLAB, C)).astype(BF16), weight_p[...])
        for half, hz, base in PIECES:
            size = WIN * SIZES[hz]
            row = ZONE_BASE[(dz, hz)] + at * size
            space[half, row : row + size, 0:C] = normed[base : base + size]
            space[half, row : row + size, C:FEED] = dcontext[base : base + size]
        if at == SIZES[dz] - 1:
            if dz == 0:
                pl.semaphore_wait(barrier, owners + batches - 2)
            for hz in range(3):
                zone = (dz, hz)
                base, rows = ZONE_BASE[zone], ZONE_ROWS[zone]
                filled = space[:, base : base + rows, :].astype(BF16)
                if zone in AHEAD:
                    send_buffers[zone][...] = filled
                    ahead(zone).start()
                else:
                    group = GROUP_LIST.index(((dz - 1), (hz - 1)))
                    x[2 * group : 2 * group + 2, 0:rows, :] = filled
    first_share().start()

    weight_t[...] = jnp.transpose(weight[...].astype(F32)).astype(BF16)
    grad[...] = jnp.zeros_like(grad)
    scale = HEAD**-0.5
    late = 1 - (lax.rem(depth, 4) + 3) // 4

    @pl.loop(0, 8)
    def _(turn):
        pair = turn // 2
        i = turn + late * pair * (3 - pair) * (3 - 2 * pair)
        for number, group in enumerate(GROUP_LIST):
            if number:

                @pl.when(i == 2 * number)
                def _():
                    for zone in GROUPS[group]:
                        if zone in AHEAD:
                            ahead(zone).wait_recv()

        @pl.when(turn == 3)
        def _():
            first_share().wait_recv()

            @pl.loop(1, batches)
            def _(step):
                next_share(step).start()

        normed = x[i, :, 0:C]
        label_row = label[i]
        label_column = jnp.transpose(jnp.broadcast_to(label_row, (8, ROWS)))[:, 0:1]
        bias[...] = jnp.where(label_column == label_row, 0.0, -1e30)
        proj[...] = nn(normed, weight[...]).astype(BF16)
        proj_t[...] = nt(weight_t[...], normed).astype(BF16)
        dcon_t[...] = nt(eye[...], x[i, :, C:FEED]).astype(BF16)
        for head in range(HEADS):
            a, b, c = (slice(k * ATTN + head * HEAD, k * ATTN + head * HEAD + HEAD) for k in range(3))
            scores = nn(proj[:, b], proj_t[a, :]) * (scale * math.log2(math.e)) + bias[...]
            exponent = jnp.exp2(scores - jnp.max(scores, axis=0, keepdims=True))
            weights = (exponent * (1.0 / jnp.sum(exponent, axis=0, keepdims=True))).astype(BF16)
            context_t = nn(proj_t[c, :], weights)
            con_t[a, :] = context_t
            inner = jnp.sum(dcon_t[a, :].astype(F32) * context_t, axis=0, keepdims=True)
            dweights = nn(proj[:, c], dcon_t[a, :])
            dscores = (weights.astype(F32) * (dweights - inner) * scale).astype(BF16)
            dproj_t[a, :] = nn(proj_t[b, :], dscores).astype(BF16)
            dproj_t[b, :] = jnp.transpose(nn(dscores, proj[:, a])).astype(BF16)
            cot = x[i, :, C + head * HEAD : C + head * HEAD + HEAD]
            dproj_t[c, :] = jnp.transpose(nn(weights, cot)).astype(BF16)
        context_w[i] = jnp.transpose(con_t[...]).astype(BF16)
        grad[...] += nn(dproj_t[...], normed)
        for number, group in enumerate(GROUP_LIST):
            if number:
                for half in range(2):

                    @pl.when(i == 2 * number + half)
                    def _():
                        for zone in GROUPS[group]:
                            if zone in AHEAD:
                                back(zone, half).start()

    spread = jnp.transpose(grad[...])
    terms[0][...] = jnp.zeros_like(terms[0])
    for o in range(owners):
        terms[0][o, 0:lines, 0 : 3 * ATTN] = spread[o * lines : (o + 1) * lines].astype(BF16)

    @pl.loop(1, owners)
    def _(step):
        term(0, step).start()

    for zone in ZONES:
        if zone not in AHEAD:
            group = GROUP_LIST.index((zone[0] - 1, zone[1] - 1))
            base, rows = ZONE_BASE[zone], ZONE_ROWS[zone]
            context_z[:, base : base + rows, :] = context_w[2 * group : 2 * group + 2, 0:rows, :]
    for zone in HALO:
        for half in range(2):
            back(zone, half).wait_recv()
    context_space[:, TOTAL:, :] = jnp.zeros((2, context_space.shape[1] - TOTAL, ATTN), F32)
    context_space[:, 0:TOTAL, :] = context_z[...].astype(F32)
    for pair in range(EDGE // 2):
        blocks = []
        for d in (2 * pair, 2 * pair + 1):
            dz, at = zone_of(d)
            for h in range(EDGE):
                pad_v[d % 2, h, 0:EDGE, :] = vol[0, d, h]
            pieces = []
            for half, hz, _ in PIECES:
                row = ZONE_BASE[(dz, hz)] + at * WIN * SIZES[hz]
                pieces.append(context_space[half, row : row + PIECE_ROWS[hz], :])
            context = nn(back_pick[...], jnp.concatenate(pieces, axis=0).astype(BF16)).astype(BF16)
            context_all[d * SLAB : (d + 1) * SLAB, :] = context
            attended = nn(context, weight_p[...]).astype(BF16)
            shown, hidden = masked_pick(cells[...], mask[d])
            tokens = nn(shown, pad_v[d % 2].reshape(SLAB, C)) + hidden * token
            block = (tokens + nn(cells[...], attended)).astype(BF16).astype(F32)
            blocks += [block[o * 56 : o * 56 + 56] for o in range(4)]
        summed = sum(blocks[1:], blocks[0])
        mean = jnp.sum(summed, axis=1, keepdims=True) * (1.0 / (8 * C))
        centered = [b - mean for b in blocks]
        squares = [b * b for b in centered]
        variance = jnp.sum(sum(squares[1:], squares[0]), axis=1, keepdims=True) * (1.0 / (8 * C))
        factor = lax.rsqrt(variance + EPS)
        for o in range(8):
            features[o, pair * 56 : pair * 56 + 56, :] = centered[o] * factor * params[2 + o : 3 + o, :]

    grad_proj = tn(context_all[...], pad_u[...].reshape(EDGE * SLAB, C))
    terms[1][...] = jnp.zeros_like(terms[1])
    per = ATTN // owners
    for o in range(owners):
        rows = grad_proj[o * per : (o + 1) * per].astype(BF16)
        terms[1][o, 0:per, 0:ATTN] = rows[:, 0:ATTN]
        terms[1][o, per : 2 * per, 0:ATTN] = rows[:, ATTN:]

    @pl.loop(1, owners)
    def _(step):
        term(1, step).start()

    @pl.loop(1, batches)
    def _(step):
        next_share(step).wait_recv()

    each = 8 // batches
    result = jnp.zeros(features.shape[1:], F32)
    for step in range(batches):
        at = lax.rem(batch - step + batches, batches) * each
        for k in range(each):
            result += nn(features[at + k].astype(BF16), other[step, k * C : (k + 1) * C, :])
    sent[0 : result.shape[0], :] = result.astype(BF16)
    sent[result.shape[0] :, :] = jnp.zeros((sent.shape[0] - result.shape[0], C), BF16)
    swap_merged().start()
    result = jnp.zeros(features.shape[1:], F32)
    for step in range(batches):
        for k in range(each):
            result += nn(features[step * each + k].astype(BF16), own[step, k * C : (k + 1) * C, :])
    merged_out[height] = result.astype(BF16)

    wide = terms[0].shape[2]
    total[:, 0:wide] = terms[0][me].astype(F32)
    total[:, wide:] = terms[1][me].astype(F32)

    @pl.loop(1, owners)
    def _(step):
        term(0, step).wait_recv()
        total[:, 0:wide] += arrived[0][step].astype(F32)

    @pl.loop(1, owners)
    def _(step):
        term(1, step).wait_recv()
        total[:, wide:] += arrived[1][step].astype(F32)

    @pl.loop(1, batches)
    def _(step):
        to_batch(step).start()

    swap_merged().wait_recv()
    merged_out[heights - 1 - height] = fetched[0 : result.shape[0], :]
    gathered[0] = total[...]

    @pl.loop(1, batches)
    def _(step):
        to_batch(step).wait_recv()
        gathered[0] += gathered[step]

    grad_qkv_out[...] = gathered[0, 0:lines, 0 : 3 * ATTN]
    grad_proj_out[:, 0:ATTN] = gathered[0, 0:per, wide : wide + ATTN]
    grad_proj_out[:, ATTN:] = gathered[0, per : 2 * per, wide : wide + ATTN]

    for zone in HALO:
        ahead(zone).wait_send()
        for half in range(2):
            back(zone, half).wait_send()
    first_share().wait_send()
    swap_merged().wait_send()

    @pl.loop(1, owners)
    def _(step):
        term(0, step).wait_send()
        term(1, step).wait_send()

    @pl.loop(1, batches)
    def _(step):
        next_share(step).wait_send()
        to_batch(step).wait_send()


def run_block(operands, sizes):
    vmem = pl.BlockSpec(memory_space=pltpu.VMEM)
    owners, batches = sizes[0] * sizes[1], sizes[2]
    lines = up(C // owners, 16)
    wide, narrow = up(3 * ATTN, 128), up(ATTN, 128)
    cell_rows = 7 * 56

    def pair_of(rows):
        return [pltpu.VMEM((rows, lines, wide), BF16), pltpu.VMEM((rows, lines, narrow), BF16)]

    return pl.pallas_call(
        functools.partial(block_kernel, sizes),
        out_shape=[
            jax.ShapeDtypeStruct((2, cell_rows, C), BF16),
            jax.ShapeDtypeStruct((C // owners, 3 * ATTN), F32),
            jax.ShapeDtypeStruct((ATTN // owners, C), F32),
        ],
        in_specs=[vmem] * len(operands),
        out_specs=[vmem] * 3,
        scratch_shapes=[
            pltpu.VMEM((8, ROWS, FEED), BF16),
            pltpu.VMEM((2, TOTAL, FEED), F32),
            pltpu.VMEM((2, EDGE, PITCH, C), BF16),
            pltpu.VMEM((EDGE, EDGE, PITCH, C), BF16),
            pltpu.VMEM((8, ROWS, ATTN), BF16),
            pltpu.VMEM((2, TOTAL, ATTN), BF16),
            pltpu.VMEM((ROWS, ROWS), F32),
            pltpu.VMEM((ROWS, 3 * ATTN), BF16),
            pltpu.VMEM((3 * ATTN, ROWS), BF16),
            pltpu.VMEM((ATTN, ROWS), BF16),
            pltpu.VMEM((ATTN, ROWS), F32),
            pltpu.VMEM((3 * ATTN, ROWS), BF16),
            pltpu.VMEM((3 * ATTN, C), BF16),
            pltpu.VMEM((3 * ATTN, C), F32),
            pltpu.VMEM((2, TOTAL + 32, ATTN), F32),
            pltpu.VMEM((EDGE * SLAB, ATTN), BF16),
            pltpu.VMEM((8, cell_rows, C), F32),
            pltpu.VMEM((batches, 8 * C // batches, C), BF16),
            pltpu.VMEM((up(cell_rows, 16), C), BF16),
            pltpu.VMEM((up(cell_rows, 16), C), BF16),
            pair_of(owners),
            pair_of(owners),
            pltpu.VMEM((lines, wide + narrow), F32),
            pltpu.VMEM((batches, lines, wide + narrow), F32),
            pltpu.SemaphoreType.DMA((5,)),
            pltpu.SemaphoreType.DMA((5,)),
            pltpu.SemaphoreType.DMA((10,)),
            pltpu.SemaphoreType.DMA((10,)),
            pltpu.SemaphoreType.DMA((batches,)),
            pltpu.SemaphoreType.DMA((batches,)),
            pltpu.SemaphoreType.DMA((1,)),
            pltpu.SemaphoreType.DMA((1,)),
            pltpu.SemaphoreType.DMA((2, owners)),
            pltpu.SemaphoreType.DMA((2, owners)),
            pltpu.SemaphoreType.DMA((batches,)),
            pltpu.SemaphoreType.DMA((batches,)),
        ]
        + [pltpu.VMEM((2, ZONE_ROWS[zone], FEED), BF16) for zone in HALO],
        cost_estimate=pl.CostEstimate(flops=80_000_000_000, bytes_accessed=12_000_000, transcendentals=8_000_000),
        compiler_params=pltpu.CompilerParams(
            collective_id=1, has_side_effects=True, vmem_limit_bytes=VMEM_LIMIT
        ),
        name="block",
    )(*operands)


def group_labels(labels, group):
    parts = []
    for zone in GROUPS[group]:
        spans = []
        for z in zone:
            start = {1: 0, 2: WIN, 0: WIN + SIZES[2]}[z]
            spans.append((start, SIZES[z]))
        (d, nd), (h, nh) = spans
        part = labels[d : d + nd, h : h + nh].reshape(nd, nh, 2, WIN).transpose(2, 0, 1, 3)
        part = part.reshape(2, nd * nh * WIN)
        parts.append(jnp.pad(part, ((0, 0), (0, ZONE_ROWS[zone] - nd * nh * WIN)), constant_values=-1))
    row = jnp.concatenate(parts, axis=1)
    row = jnp.pad(row, ((0, 0), (0, ROWS - row.shape[1])), constant_values=-1)
    return row.reshape(2, 1, ROWS).astype(F32)


def shards(
    volume,
    patch_mask,
    mask_token,
    labels,
    norm_gain,
    qkv_weight,
    proj_weight,
    merge_gain,
    merge_weight,
    upstream,
):
    sizes = tuple(lax.axis_size(n) for n in ("depth", "height", "batch"))
    pick = slab_to_pieces()
    mask = jnp.pad(patch_mask[0], ((0, 0), (0, 0), (0, PITCH - EDGE))).reshape(EDGE, 1, SLAB).astype(BF16)
    label = jnp.concatenate([group_labels(labels[0], group) for group in GROUP_LIST], 0)
    params = jnp.concatenate((norm_gain, mask_token.astype(F32), merge_gain)).reshape(10, C)
    operands = (
        volume,
        upstream,
        mask,
        label,
        jnp.asarray(pick, BF16),
        jnp.asarray(pick.T, BF16),
        jnp.asarray(slab_to_cells(), BF16),
        params,
        qkv_weight,
        proj_weight,
        jnp.asarray(np.eye(ATTN), BF16),
        merge_weight.reshape(sizes[2], -1, C),
    )
    merged, grad_qkv, grad_proj = run_block(operands, sizes)
    merged = merged.reshape(2, 7, 7, 8, C)[:, :, :, :7].transpose(1, 0, 2, 3, 4).reshape(1, 7, 14, 7, C)
    return (merged, grad_qkv, grad_proj)


def solution(mesh):
    return jax.shard_map(
        shards,
        mesh=mesh,
        in_specs=(
            P("batch", "depth", "height", None, None),
            P("batch", "depth", "height", None),
            P(),
            P("batch", "depth", "height", None),
            P(),
            P(),
            P(),
            P(),
            P(None, "height"),
            P("batch", "depth", "height", None, None),
        ),
        out_specs=(
            P("batch", "depth", None, None, "height"),
            P(("depth", "height"), None),
            P(("depth", "height"), None),
        ),
        check_vma=False,
    )
```

```python
import functools
import math

import jax
import jax.numpy as jnp
import numpy as np
from jax import lax
from jax.experimental import pallas as pl
from jax.experimental.pallas import tpu as pltpu
from jax.sharding import PartitionSpec as P

HEADS = 6
HEAD = 32
ATTN = 192
C = 384
WIN = 7
SHIFT = 3
EDGE = 14
PITCH = 16
SLAB = EDGE * PITCH
ROWS = 384
FEED = C + ATTN
EPS = 1e-05
F32 = jnp.float32
BF16 = jnp.bfloat16
MESH = pl.DeviceIdType.MESH
VMEM_LIMIT = 56 * 2**20

SIZES = (3, 7, 4)
FIRST = (0, 3, 10)
ZONES = [(a, b) for a in range(3) for b in range(3)]


def up(value, unit):
    return -(-value // unit) * unit


ZONE_ROWS = {z: up(WIN * SIZES[z[0]] * SIZES[z[1]], 16) for z in ZONES}
ZONE_BASE = {}
TOTAL = 0
for zone in ZONES:
    ZONE_BASE[zone] = TOTAL
    TOTAL += ZONE_ROWS[zone]
PIECE_ROWS = tuple(up(WIN * s, 8) for s in SIZES)
PIECES = []
_at = 0
for _half in range(2):
    for _hz in range(3):
        PIECES.append((_half, _hz, _at))
        _at += PIECE_ROWS[_hz]

GROUPS = {
    (0, 0): ((1, 1),),
    (0, 1): ((1, 2), (1, 0)),
    (1, 0): ((2, 1), (0, 1)),
    (1, 1): ((2, 2), (2, 0), (0, 2), (0, 0)),
}


def slab_to_pieces():
    pick = np.zeros((SLAB, SLAB), np.float32)
    for half, hz, base in PIECES:
        for hh in range(SIZES[hz]):
            for k in range(WIN):
                width = (SHIFT + WIN * half + k) % EDGE
                pick[base + hh * WIN + k, (FIRST[hz] + hh) * PITCH + width] = 1
    return pick


def slab_to_cells():
    pick = np.zeros((SLAB, SLAB), np.float32)
    for hh in range(2):
        for ww in range(2):
            for h in range(7):
                for w in range(7):
                    pick[(hh * 2 + ww) * 56 + h * 8 + w, (2 * h + hh) * PITCH + 2 * w + ww] = 1
    return pick


def nn(a, b):
    return jnp.dot(a, b, preferred_element_type=F32)


def nt(a, b):
    return lax.dot_general(a, b, (((1,), (1,)), ((), ())), preferred_element_type=F32)


def tn(a, b):
    return lax.dot_general(a, b, (((0,), (0,)), ((), ())), preferred_element_type=F32)


def masked_pick(pick, mask_row):
    hidden = pick * mask_row
    return pick - hidden, jnp.sum(hidden.astype(F32), axis=1, keepdims=True)


AHEAD = {}
for _group, _members in GROUPS.items():
    _row = 0
    for zone in _members:
        if 0 in zone:
            AHEAD[zone] = (_group, _row)
        _row += ZONE_ROWS[zone]
HALO = list(AHEAD)
GROUP_LIST = list(GROUPS)


def neighbour(zone, by, sizes):
    device = {}
    for axis, part, size in zip(("depth", "height"), zone, sizes):
        if part == 0:
            device[axis] = lax.rem(lax.axis_index(axis) + by + size, size)
    return device


def zone_of(d):
    dz = 0 if d < FIRST[1] else 1 if d < FIRST[2] else 2
    return dz, d - FIRST[dz]


def block_kernel(sizes, *refs):
    depths, heights, batches = sizes
    owners = depths * heights
    lines = C // owners
    vol, ups, mask, label, pick, back_pick, cells, params, weight, weight_p, eye, own = refs[:12]
    merged_out, grad_qkv_out, grad_proj_out = refs[12:15]
    x, space, pad_v, pad_u, context_w, context_z, bias, proj, proj_t, dcon_t, con_t, dproj_t = refs[15:27]
    weight_t, grad, context_space, context_all, features, other, sent, fetched = refs[27:35]
    terms, landed, partial, ahead_send, ahead_recv, back_send, back_recv = refs[35:42]
    share_send, share_recv, merged_send, merged_recv, term_send, term_recv = refs[42:48]
    send_buffers = dict(zip(HALO, refs[48:53]))

    depth, height, batch = (lax.axis_index(n) for n in ("depth", "height", "batch"))
    me = depth * heights + height
    peer = {"height": heights - 1 - height}

    across = min(depths, 4)
    planes = owners // across
    across_at = lax.rem(depth, across)
    plane_at = depth // across * heights + height

    def owner_at(step):
        to = lax.rem(me + step, owners)
        return {"depth": to // heights, "height": lax.rem(to, heights)}

    def member(stage, place):
        if stage == 0:
            return {"depth": depth // across * across + place}
        if stage == 1:
            return {"depth": place // heights * across + across_at, "height": lax.rem(place, heights)}
        return {"batch": place}

    def batch_at(step):
        return {"batch": lax.rem(batch + step, batches)}

    def remote(src, dst, send, recv, device):
        return pltpu.make_async_remote_copy(
            src_ref=src, dst_ref=dst, send_sem=send, recv_sem=recv, device_id=device, device_id_type=MESH
        )

    def ahead(zone):
        group, row = AHEAD[zone]
        slot = HALO.index(zone)
        landing = x.at[pl.ds(2 * GROUP_LIST.index(group), 2), pl.ds(row, ZONE_ROWS[zone]), :]
        return remote(
            send_buffers[zone], landing, ahead_send.at[slot], ahead_recv.at[slot], neighbour(zone, -1, sizes)
        )

    def back(zone, half):
        group, row = AHEAD[zone]
        slot = 2 * HALO.index(zone) + half
        return remote(
            context_w.at[2 * GROUP_LIST.index(group) + half, pl.ds(row, ZONE_ROWS[zone]), :],
            context_z.at[half, pl.ds(ZONE_BASE[zone], ZONE_ROWS[zone]), :],
            back_send.at[slot],
            back_recv.at[slot],
            neighbour(zone, 1, sizes),
        )

    def first_share():
        return remote(own.at[batch], other.at[0], share_send.at[0], share_recv.at[0], peer)

    def pass_share():
        before = {"depth": lax.rem(depth + depths - 1, depths)}
        return remote(other.at[0], other.at[0], share_send.at[batches], share_recv.at[0], before)

    def next_share(step):
        return remote(other.at[0], other.at[step], share_send.at[step], share_recv.at[step], batch_at(step))

    def swap_merged():
        return remote(sent, fetched, merged_send.at[0], merged_recv.at[0], peer)

    places = (across_at, plane_at, batch)
    counts = (across, planes, batches)

    def exchange(stage, kind, step):
        place = lax.rem(places[stage] + step, counts[stage])
        source = (terms[kind].at[place], partial[0][kind].at[place], partial[1][kind])[stage]
        slot = sum(counts[:stage]) + step
        return remote(
            source,
            landed[stage][kind].at[step],
            term_send.at[kind, slot],
            term_recv.at[kind, slot],
            member(stage, place),
        )

    def begin(stage, kind):
        @pl.loop(1, counts[stage])
        def _(step):
            exchange(stage, kind, step).start()

    def finish(stage, kind):
        out = partial[stage][kind]
        if stage == 0:
            out[...] = terms[kind][across_at].astype(F32)
        elif stage == 1:
            out[...] = partial[0][kind][plane_at]
        else:
            out[...] = partial[1][kind][...]

        @pl.loop(1, counts[stage])
        def _(step):
            exchange(stage, kind, step).wait_recv()
            out[...] += landed[stage][kind][step].astype(F32)

    barrier = pltpu.get_barrier_semaphore()

    @pl.loop(1, owners)
    def _(step):
        pl.semaphore_signal(barrier, inc=1, device_id=owner_at(step), device_id_type=MESH)

    @pl.loop(1, batches)
    def _(step):
        pl.semaphore_signal(barrier, inc=1, device_id=batch_at(step), device_id_type=MESH)

    gain, token = params[0:1, :], params[1:2, :]
    space[...] = jnp.zeros_like(space)
    pad_v[...] = jnp.zeros_like(pad_v)
    pad_u[...] = jnp.zeros_like(pad_u)
    for number, group in enumerate(GROUP_LIST):
        used = sum(ZONE_ROWS[zone] for zone in GROUPS[group])
        x[2 * number : 2 * number + 2, used:, :] = jnp.zeros((2, ROWS - used, FEED), BF16)
    for d in range(EDGE):
        dz, at = zone_of(d)
        for h in range(EDGE):
            pad_v[d % 2, h, 0:EDGE, :] = vol[0, d, h]
            pad_u[d, h, 0:EDGE, :] = ups[0, d, h]
        shown, hidden = masked_pick(pick[...], mask[d])
        tokens = nn(shown, pad_v[d % 2].reshape(SLAB, C)) + hidden * token
        mean = jnp.mean(tokens, axis=1, keepdims=True)
        centered = tokens - mean
        variance = jnp.mean(centered * centered, axis=1, keepdims=True)
        normed = centered * lax.rsqrt(variance + EPS) * gain
        dcontext = nt(nn(pick[...], pad_u[d].reshape(SLAB, C)).astype(BF16), weight_p[...])
        for half, hz, base in PIECES:
            size = WIN * SIZES[hz]
            row = ZONE_BASE[(dz, hz)] + at * size
            space[half, row : row + size, 0:C] = normed[base : base + size]
            space[half, row : row + size, C:FEED] = dcontext[base : base + size]
        if at == SIZES[dz] - 1:
            if dz == 0:
                pl.semaphore_wait(barrier, owners + batches - 2)
            for hz in range(3):
                zone = (dz, hz)
                base, rows = ZONE_BASE[zone], ZONE_ROWS[zone]
                filled = space[:, base : base + rows, :].astype(BF16)
                if zone in AHEAD:
                    send_buffers[zone][...] = filled
                    ahead(zone).start()
                else:
                    group = GROUP_LIST.index(((dz - 1), (hz - 1)))
                    x[2 * group : 2 * group + 2, 0:rows, :] = filled
    late = 1 - (lax.rem(depth, 4) + 3) // 4

    @pl.when(late == 0)
    def _():
        first_share().start()

    weight_t[...] = jnp.transpose(weight[...].astype(F32)).astype(BF16)
    grad[...] = jnp.zeros_like(grad)
    scale = HEAD**-0.5

    @pl.loop(0, 8)
    def _(turn):
        pair = turn // 2
        i = turn + late * pair * (3 - pair) * (3 - 2 * pair)
        for number, group in enumerate(GROUP_LIST):
            if number:

                @pl.when(i == 2 * number)
                def _():
                    for zone in GROUPS[group]:
                        if zone in AHEAD:
                            ahead(zone).wait_recv()

        @pl.when(turn == 3 + 2 * late)
        def _():
            first_share().wait_recv()

            @pl.when(lax.rem(depth, 4) == 1)
            def _():
                pass_share().start()

            @pl.loop(1, batches)
            def _(step):
                next_share(step).start()

        normed = x[i, :, 0:C]
        label_row = label[i]
        label_column = jnp.transpose(jnp.broadcast_to(label_row, (8, ROWS)))[:, 0:1]
        bias[...] = jnp.where(label_column == label_row, 0.0, -1e30)
        proj[...] = nn(normed, weight[...]).astype(BF16)
        proj_t[...] = nt(weight_t[...], normed).astype(BF16)
        dcon_t[...] = nt(eye[...], x[i, :, C:FEED]).astype(BF16)
        for head in range(HEADS):
            a, b, c = (slice(k * ATTN + head * HEAD, k * ATTN + head * HEAD + HEAD) for k in range(3))
            scores = nn(proj[:, b], proj_t[a, :]) * (scale * math.log2(math.e)) + bias[...]
            exponent = jnp.exp2(scores - jnp.max(scores, axis=0, keepdims=True))
            weights = (exponent * (1.0 / jnp.sum(exponent, axis=0, keepdims=True))).astype(BF16)
            context_t = nn(proj_t[c, :], weights)
            con_t[a, :] = context_t
            inner = jnp.sum(dcon_t[a, :].astype(F32) * context_t, axis=0, keepdims=True)
            dweights = nn(proj[:, c], dcon_t[a, :])
            dscores = (weights.astype(F32) * (dweights - inner) * scale).astype(BF16)
            dproj_t[a, :] = nn(proj_t[b, :], dscores).astype(BF16)
            dproj_t[b, :] = jnp.transpose(nn(dscores, proj[:, a])).astype(BF16)
            cot = x[i, :, C + head * HEAD : C + head * HEAD + HEAD]
            dproj_t[c, :] = jnp.transpose(nn(weights, cot)).astype(BF16)
        context_w[i] = jnp.transpose(con_t[...]).astype(BF16)
        grad[...] += nn(dproj_t[...], normed)
        for number, group in enumerate(GROUP_LIST):
            if number:
                for half in range(2):

                    @pl.when(i == 2 * number + half)
                    def _():
                        for zone in GROUPS[group]:
                            if zone in AHEAD:
                                back(zone, half).start()

    def place_of(owner):
        return owner // heights % across, owner // heights // across * heights + owner % heights

    spread = jnp.transpose(grad[...])
    terms[0][...] = jnp.zeros_like(terms[0])
    for o in range(owners):
        terms[0][*place_of(o), 0:lines, 0 : 3 * ATTN] = spread[o * lines : (o + 1) * lines].astype(BF16)
    begin(0, 0)

    for zone in ZONES:
        if zone not in AHEAD:
            group = GROUP_LIST.index((zone[0] - 1, zone[1] - 1))
            base, rows = ZONE_BASE[zone], ZONE_ROWS[zone]
            context_z[:, base : base + rows, :] = context_w[2 * group : 2 * group + 2, 0:rows, :]
    context_space[:, TOTAL:, :] = jnp.zeros((2, context_space.shape[1] - TOTAL, ATTN), F32)

    def restore(dz):
        start, stop = ZONE_BASE[(dz, 0)], ZONE_BASE[(dz, 2)] + ZONE_ROWS[(dz, 2)]
        context_space[:, start:stop, :] = context_z[:, start:stop, :].astype(F32)
        for at in range(SIZES[dz]):
            d = FIRST[dz] + at
            pieces = []
            for half, hz, _ in PIECES:
                row = ZONE_BASE[(dz, hz)] + at * WIN * SIZES[hz]
                pieces.append(context_space[half, row : row + PIECE_ROWS[hz], :])
            context = nn(back_pick[...], jnp.concatenate(pieces, axis=0).astype(BF16))
            context_all[d * SLAB : (d + 1) * SLAB, :] = context.astype(BF16)

    for dz in (1, 2, 0):
        for zone in HALO:
            if zone[0] == dz:
                for half in range(2):
                    back(zone, half).wait_recv()
        restore(dz)

    grad_proj = tn(context_all[...], pad_u[...].reshape(EDGE * SLAB, C))
    terms[1][...] = jnp.zeros_like(terms[1])
    per = ATTN // owners
    for o in range(owners):
        rows = grad_proj[o * per : (o + 1) * per].astype(BF16)
        terms[1][*place_of(o), 0:per, 0:ATTN] = rows[:, 0:ATTN]
        terms[1][*place_of(o), per : 2 * per, 0:ATTN] = rows[:, ATTN:]
    begin(0, 1)

    def merge_pair(pair):
        blocks = []
        for d in (2 * pair, 2 * pair + 1):
            for h in range(EDGE):
                pad_v[d % 2, h, 0:EDGE, :] = vol[0, d, h]
            attended = nn(context_all[d * SLAB : (d + 1) * SLAB, :], weight_p[...]).astype(BF16)
            shown, hidden = masked_pick(cells[...], mask[d])
            tokens = nn(shown, pad_v[d % 2].reshape(SLAB, C)) + hidden * token
            block = (tokens + nn(cells[...], attended)).astype(BF16).astype(F32)
            blocks += [block[o * 56 : o * 56 + 56] for o in range(4)]
        summed = sum(blocks[1:], blocks[0])
        mean = jnp.sum(summed, axis=1, keepdims=True) * (1.0 / (8 * C))
        centered = [b - mean for b in blocks]
        squares = [b * b for b in centered]
        variance = jnp.sum(sum(squares[1:], squares[0]), axis=1, keepdims=True) * (1.0 / (8 * C))
        factor = lax.rsqrt(variance + EPS)
        for o in range(8):
            features[o, pair * 56 : pair * 56 + 56, :] = centered[o] * factor * params[2 + o : 3 + o, :]

    for pair in range(4):
        merge_pair(pair)
    finish(0, 0)
    begin(1, 0)
    for pair in range(4, EDGE // 2):
        merge_pair(pair)
    finish(0, 1)
    begin(1, 1)

    @pl.loop(1, batches)
    def _(step):
        next_share(step).wait_recv()

    each = 8 // batches
    result = jnp.zeros(features.shape[1:], F32)
    for step in range(batches):
        at = lax.rem(batch - step + batches, batches) * each
        for k in range(each):
            result += nn(features[at + k].astype(BF16), other[step, k * C : (k + 1) * C, :])
    sent[0 : result.shape[0], :] = result.astype(BF16)
    sent[result.shape[0] :, :] = jnp.zeros((sent.shape[0] - result.shape[0], C), BF16)
    swap_merged().start()
    for kind in range(2):
        finish(1, kind)
        begin(2, kind)
    result = jnp.zeros(features.shape[1:], F32)
    for step in range(batches):
        for k in range(each):
            result += nn(features[step * each + k].astype(BF16), own[step, k * C : (k + 1) * C, :])
    merged_out[height] = result.astype(BF16)
    for kind in range(2):
        finish(2, kind)
    sums = partial[2]
    grad_qkv_out[...] = sums[0][0:lines, 0 : 3 * ATTN]
    grad_proj_out[:, 0:ATTN] = sums[1][0:per, 0:ATTN]
    grad_proj_out[:, ATTN:] = sums[1][per : 2 * per, 0:ATTN]
    swap_merged().wait_recv()
    merged_out[heights - 1 - height] = fetched[0 : result.shape[0], :]

    for zone in HALO:
        ahead(zone).wait_send()
        for half in range(2):
            back(zone, half).wait_send()

    @pl.when(late == 0)
    def _():
        first_share().wait_send()

    @pl.when(lax.rem(depth, 4) == 1)
    def _():
        pass_share().wait_send()

    swap_merged().wait_send()

    @pl.loop(1, batches)
    def _(step):
        next_share(step).wait_send()

    for stage in range(3):
        for kind in range(2):

            @pl.loop(1, counts[stage])
            def _(step):
                exchange(stage, kind, step).wait_send()


def run_block(operands, sizes):
    vmem = pl.BlockSpec(memory_space=pltpu.VMEM)
    owners, batches = sizes[0] * sizes[1], sizes[2]
    lines = up(C // owners, 16)
    wide, narrow = up(3 * ATTN, 128), up(ATTN, 128)
    cell_rows = 7 * 56

    across = min(sizes[0], 4)
    planes = owners // across

    def pair_of(kind, *shape):
        return [pltpu.VMEM(shape + (lines, wide), kind), pltpu.VMEM(shape + (lines, narrow), kind)]

    exchanges = across + planes + batches

    return pl.pallas_call(
        functools.partial(block_kernel, sizes),
        out_shape=[
            jax.ShapeDtypeStruct((2, cell_rows, C), BF16),
            jax.ShapeDtypeStruct((C // owners, 3 * ATTN), F32),
            jax.ShapeDtypeStruct((ATTN // owners, C), F32),
        ],
        in_specs=[vmem] * len(operands),
        out_specs=[vmem] * 3,
        scratch_shapes=[
            pltpu.VMEM((8, ROWS, FEED), BF16),
            pltpu.VMEM((2, TOTAL, FEED), F32),
            pltpu.VMEM((2, EDGE, PITCH, C), BF16),
            pltpu.VMEM((EDGE, EDGE, PITCH, C), BF16),
            pltpu.VMEM((8, ROWS, ATTN), BF16),
            pltpu.VMEM((2, TOTAL, ATTN), BF16),
            pltpu.VMEM((ROWS, ROWS), F32),
            pltpu.VMEM((ROWS, 3 * ATTN), BF16),
            pltpu.VMEM((3 * ATTN, ROWS), BF16),
            pltpu.VMEM((ATTN, ROWS), BF16),
            pltpu.VMEM((ATTN, ROWS), F32),
            pltpu.VMEM((3 * ATTN, ROWS), BF16),
            pltpu.VMEM((3 * ATTN, C), BF16),
            pltpu.VMEM((3 * ATTN, C), F32),
            pltpu.VMEM((2, TOTAL + 32, ATTN), F32),
            pltpu.VMEM((EDGE * SLAB, ATTN), BF16),
            pltpu.VMEM((8, cell_rows, C), F32),
            pltpu.VMEM((batches, 8 * C // batches, C), BF16),
            pltpu.VMEM((up(cell_rows, 16), C), BF16),
            pltpu.VMEM((up(cell_rows, 16), C), BF16),
            pair_of(BF16, across, planes),
            [pair_of(BF16, across, planes), pair_of(F32, planes), pair_of(F32, batches)],
            [pair_of(F32, planes), pair_of(F32), pair_of(F32)],
            pltpu.SemaphoreType.DMA((5,)),
            pltpu.SemaphoreType.DMA((5,)),
            pltpu.SemaphoreType.DMA((10,)),
            pltpu.SemaphoreType.DMA((10,)),
            pltpu.SemaphoreType.DMA((batches + 1,)),
            pltpu.SemaphoreType.DMA((batches,)),
            pltpu.SemaphoreType.DMA((1,)),
            pltpu.SemaphoreType.DMA((1,)),
            pltpu.SemaphoreType.DMA((2, exchanges)),
            pltpu.SemaphoreType.DMA((2, exchanges)),
        ]
        + [pltpu.VMEM((2, ZONE_ROWS[zone], FEED), BF16) for zone in HALO],
        cost_estimate=pl.CostEstimate(flops=80_000_000_000, bytes_accessed=12_000_000, transcendentals=8_000_000),
        compiler_params=pltpu.CompilerParams(
            collective_id=1, has_side_effects=True, vmem_limit_bytes=VMEM_LIMIT
        ),
        name="block",
    )(*operands)


def group_labels(labels, group):
    parts = []
    for zone in GROUPS[group]:
        spans = []
        for z in zone:
            start = {1: 0, 2: WIN, 0: WIN + SIZES[2]}[z]
            spans.append((start, SIZES[z]))
        (d, nd), (h, nh) = spans
        part = labels[d : d + nd, h : h + nh].reshape(nd, nh, 2, WIN).transpose(2, 0, 1, 3)
        part = part.reshape(2, nd * nh * WIN)
        parts.append(jnp.pad(part, ((0, 0), (0, ZONE_ROWS[zone] - nd * nh * WIN)), constant_values=-1))
    row = jnp.concatenate(parts, axis=1)
    row = jnp.pad(row, ((0, 0), (0, ROWS - row.shape[1])), constant_values=-1)
    return row.reshape(2, 1, ROWS).astype(F32)


def shards(
    volume,
    patch_mask,
    mask_token,
    labels,
    norm_gain,
    qkv_weight,
    proj_weight,
    merge_gain,
    merge_weight,
    upstream,
):
    sizes = tuple(lax.axis_size(n) for n in ("depth", "height", "batch"))
    pick = slab_to_pieces()
    mask = jnp.pad(patch_mask[0], ((0, 0), (0, 0), (0, PITCH - EDGE))).reshape(EDGE, 1, SLAB).astype(BF16)
    label = jnp.concatenate([group_labels(labels[0], group) for group in GROUP_LIST], 0)
    params = jnp.concatenate((norm_gain, mask_token.astype(F32), merge_gain)).reshape(10, C)
    operands = (
        volume,
        upstream,
        mask,
        label,
        jnp.asarray(pick, BF16),
        jnp.asarray(pick.T, BF16),
        jnp.asarray(slab_to_cells(), BF16),
        params,
        qkv_weight,
        proj_weight,
        jnp.asarray(np.eye(ATTN), BF16),
        merge_weight.reshape(sizes[2], -1, C),
    )
    merged, grad_qkv, grad_proj = run_block(operands, sizes)
    merged = merged.reshape(2, 7, 7, 8, C)[:, :, :, :7].transpose(1, 0, 2, 3, 4).reshape(1, 7, 14, 7, C)
    return (merged, grad_qkv, grad_proj)


def solution(mesh):
    return jax.shard_map(
        shards,
        mesh=mesh,
        in_specs=(
            P("batch", "depth", "height", None, None),
            P("batch", "depth", "height", None),
            P(),
            P("batch", "depth", "height", None),
            P(),
            P(),
            P(),
            P(),
            P(None, "height"),
            P("batch", "depth", "height", None, None),
        ),
        out_specs=(
            P("batch", "depth", None, None, "height"),
            P(("depth", "height"), None),
            P(("depth", "height"), None),
        ),
        check_vma=False,
    )
```

```python
import functools
import math

import jax
import jax.numpy as jnp
import numpy as np
from jax import lax
from jax.experimental import pallas as pl
from jax.experimental.pallas import tpu as pltpu
from jax.sharding import PartitionSpec as P

HEADS = 6
HEAD = 32
ATTN = 192
C = 384
WIN = 7
SHIFT = 3
EDGE = 14
PITCH = 16
SLAB = EDGE * PITCH
ROWS = 384
FEED = C + ATTN
EPS = 1e-05
F32 = jnp.float32
BF16 = jnp.bfloat16
MESH = pl.DeviceIdType.MESH
VMEM_LIMIT = 56 * 2**20

SIZES = (3, 7, 4)
FIRST = (0, 3, 10)
ZONES = [(a, b) for a in range(3) for b in range(3)]


def up(value, unit):
    return -(-value // unit) * unit


ZONE_ROWS = {z: up(WIN * SIZES[z[0]] * SIZES[z[1]], 16) for z in ZONES}
ZONE_BASE = {}
TOTAL = 0
for zone in ZONES:
    ZONE_BASE[zone] = TOTAL
    TOTAL += ZONE_ROWS[zone]
PIECE_ROWS = tuple(up(WIN * s, 8) for s in SIZES)
PIECES = []
_at = 0
for _half in range(2):
    for _hz in range(3):
        PIECES.append((_half, _hz, _at))
        _at += PIECE_ROWS[_hz]

GROUPS = {
    (0, 0): ((1, 1),),
    (0, 1): ((1, 2), (1, 0)),
    (1, 0): ((2, 1), (0, 1)),
    (1, 1): ((2, 2), (2, 0), (0, 2), (0, 0)),
}


def slab_to_pieces():
    pick = np.zeros((SLAB, SLAB), np.float32)
    for half, hz, base in PIECES:
        for hh in range(SIZES[hz]):
            for k in range(WIN):
                width = (SHIFT + WIN * half + k) % EDGE
                pick[base + hh * WIN + k, (FIRST[hz] + hh) * PITCH + width] = 1
    return pick


def slab_to_cells():
    pick = np.zeros((SLAB, SLAB), np.float32)
    for hh in range(2):
        for ww in range(2):
            for h in range(7):
                for w in range(7):
                    pick[(hh * 2 + ww) * 56 + h * 8 + w, (2 * h + hh) * PITCH + 2 * w + ww] = 1
    return pick


def nn(a, b):
    return jnp.dot(a, b, preferred_element_type=F32)


def nt(a, b):
    return lax.dot_general(a, b, (((1,), (1,)), ((), ())), preferred_element_type=F32)


def tn(a, b):
    return lax.dot_general(a, b, (((0,), (0,)), ((), ())), preferred_element_type=F32)


def masked_pick(pick, mask_row):
    hidden = pick * mask_row
    return pick - hidden, jnp.sum(hidden.astype(F32), axis=1, keepdims=True)


AHEAD = {}
for _group, _members in GROUPS.items():
    _row = 0
    for zone in _members:
        if 0 in zone:
            AHEAD[zone] = (_group, _row)
        _row += ZONE_ROWS[zone]
HALO = list(AHEAD)
DEEP = [(0, 1), (0, 2)]
LATER = [(2, 0), (0, 2), (0, 0)]
GROUP_LIST = list(GROUPS)


def neighbour(zone, by, sizes):
    device = {}
    for axis, part, size in zip(("depth", "height"), zone, sizes):
        if part == 0:
            device[axis] = lax.rem(lax.axis_index(axis) + by + size, size)
    return device


def zone_of(d):
    dz = 0 if d < FIRST[1] else 1 if d < FIRST[2] else 2
    return dz, d - FIRST[dz]


def block_kernel(sizes, *refs):
    depths, heights, batches = sizes
    owners = depths * heights
    lines = C // owners
    vol, ups, mask, label, pick, back_pick, cells, params, weight_t, weight_p, eye, own = refs[:12]
    merged_out, grad_qkv_out, grad_proj_out = refs[12:15]
    x, space, pad_v, pad_u, context_w, context_z, bias, proj, proj_t, dcon_t, con_t, dproj_t = refs[15:27]
    grad, context_space, context_all, features, other, sent, fetched = refs[27:34]
    terms, landed, partial, ahead_send, ahead_recv, back_send, back_recv = refs[34:41]
    share_send, share_recv, merged_send, merged_recv, term_send, term_recv = refs[41:47]
    send_buffers = dict(zip(HALO, refs[47:52]))
    score_all, weight_all, dscore_all, weight, relay_send, relay_recv = refs[52:58]
    relay_buffers = dict(zip(DEEP, refs[58:60]))

    depth, height, batch = (lax.axis_index(n) for n in ("depth", "height", "batch"))
    me = depth * heights + height
    peer = {"height": heights - 1 - height}

    across = min(depths, 4)
    planes = owners // across
    across_at = lax.rem(depth, across)
    plane_at = depth // across * heights + height

    def owner_at(step):
        to = lax.rem(me + step, owners)
        return {"depth": to // heights, "height": lax.rem(to, heights)}

    def member(stage, place):
        if stage == 0:
            return {"depth": depth // across * across + place}
        if stage == 1:
            return {"depth": place // heights * across + across_at, "height": lax.rem(place, heights)}
        return {"batch": place}

    def batch_at(step):
        return {"batch": lax.rem(batch + step, batches)}

    def remote(src, dst, send, recv, device):
        return pltpu.make_async_remote_copy(
            src_ref=src, dst_ref=dst, send_sem=send, recv_sem=recv, device_id=device, device_id_type=MESH
        )

    relayed = depths % 4 == 0 and depths > 4
    along = lax.rem(depth, 4)
    late = 1 - (along + 3) // 4

    def landing(zone, half):
        group, row = AHEAD[zone]
        return x.at[2 * GROUP_LIST.index(group) + half, pl.ds(row, ZONE_ROWS[zone]), :]

    def ahead(zone, half):
        slot = 2 * HALO.index(zone) + half
        return remote(
            send_buffers[zone].at[half],
            landing(zone, half),
            ahead_send.at[slot],
            ahead_recv.at[slot],
            neighbour(zone, -1, sizes),
        )

    def to_relay(zone):
        slot = DEEP.index(zone)
        return remote(
            send_buffers[zone].at[1],
            relay_buffers[zone],
            ahead_send.at[2 * HALO.index(zone) + 1],
            relay_recv.at[slot],
            {"depth": lax.rem(depth + 3, depths)},
        )

    def from_relay(zone):
        return remote(
            relay_buffers[zone],
            landing(zone, 1),
            relay_send.at[DEEP.index(zone)],
            ahead_recv.at[2 * HALO.index(zone) + 1],
            {"depth": lax.rem(depth + depths - 4, depths)},
        )

    def send_ahead(zone):
        ahead(zone, 0).start()
        if relayed and zone in DEEP:

            @pl.when(late == 1)
            def _():
                to_relay(zone).start()

            @pl.when(late == 0)
            def _():
                ahead(zone, 1).start()
        else:
            ahead(zone, 1).start()

    def pass_on(zone):
        if relayed:

            @pl.when(along == 3)
            def _():
                to_relay(zone).wait_recv()
                from_relay(zone).start()

    def back(zone, half):
        group, row = AHEAD[zone]
        slot = 2 * HALO.index(zone) + half
        return remote(
            context_w.at[2 * GROUP_LIST.index(group) + half, pl.ds(row, ZONE_ROWS[zone]), :],
            context_z.at[half, pl.ds(ZONE_BASE[zone], ZONE_ROWS[zone]), :],
            back_send.at[slot],
            back_recv.at[slot],
            neighbour(zone, 1, sizes),
        )

    def first_share():
        return remote(own.at[batch], other.at[0], share_send.at[0], share_recv.at[0], peer)

    def pass_share():
        before = {"depth": lax.rem(depth + depths - 1, depths)}
        return remote(other.at[0], other.at[0], share_send.at[batches], share_recv.at[0], before)

    def next_share(step):
        return remote(other.at[0], other.at[step], share_send.at[step], share_recv.at[step], batch_at(step))

    def swap_merged():
        return remote(sent, fetched, merged_send.at[0], merged_recv.at[0], peer)

    places = (across_at, plane_at, batch)
    counts = (across, planes, batches)

    def exchange(stage, kind, step):
        place = lax.rem(places[stage] + step, counts[stage])
        source = (terms[kind].at[place], partial[0][kind].at[place], partial[1][kind])[stage]
        slot = sum(counts[:stage]) + step
        return remote(
            source,
            landed[stage][kind].at[step],
            term_send.at[kind, slot],
            term_recv.at[kind, slot],
            member(stage, place),
        )

    def begin(stage, kind):
        @pl.loop(1, counts[stage])
        def _(step):
            exchange(stage, kind, step).start()

    def finish(stage, kind):
        out = partial[stage][kind]
        if stage == 0:
            out[...] = terms[kind][across_at].astype(F32)
        elif stage == 1:
            out[...] = partial[0][kind][plane_at]
        else:
            out[...] = partial[1][kind][...]

        @pl.loop(1, counts[stage])
        def _(step):
            exchange(stage, kind, step).wait_recv()
            out[...] += landed[stage][kind][step].astype(F32)

    barrier = pltpu.get_barrier_semaphore()

    @pl.loop(1, owners)
    def _(step):
        pl.semaphore_signal(barrier, inc=1, device_id=owner_at(step), device_id_type=MESH)

    @pl.loop(1, batches)
    def _(step):
        pl.semaphore_signal(barrier, inc=1, device_id=batch_at(step), device_id_type=MESH)

    gain, token = params[0:1, :], params[1:2, :]
    space[...] = jnp.zeros_like(space)
    pad_v[...] = jnp.zeros_like(pad_v)
    pad_u[...] = jnp.zeros_like(pad_u)
    for number, group in enumerate(GROUP_LIST):
        used = sum(ZONE_ROWS[zone] for zone in GROUPS[group])
        x[2 * number : 2 * number + 2, used:, :] = jnp.zeros((2, ROWS - used, FEED), BF16)
    for d in range(EDGE):
        dz, at = zone_of(d)
        for h in range(EDGE):
            pad_v[d, h, 0:EDGE, :] = vol[0, d, h]
            pad_u[d, h, 0:EDGE, :] = ups[0, d, h]
        shown, hidden = masked_pick(pick[...], mask[d])
        tokens = nn(shown, pad_v[d].reshape(SLAB, C)) + hidden * token
        mean = jnp.mean(tokens, axis=1, keepdims=True)
        centered = tokens - mean
        variance = jnp.mean(centered * centered, axis=1, keepdims=True)
        normed = centered * lax.rsqrt(variance + EPS) * gain
        dcontext = nt(nn(pick[...], pad_u[d].reshape(SLAB, C)).astype(BF16), weight_p[...])
        for half, hz, base in PIECES:
            size = WIN * SIZES[hz]
            row = ZONE_BASE[(dz, hz)] + at * size
            space[half, row : row + size, 0:C] = normed[base : base + size]
            space[half, row : row + size, C:FEED] = dcontext[base : base + size]
        if at == SIZES[dz] - 1:
            if dz == 0:
                pl.semaphore_wait(barrier, owners + batches - 2)
            for hz in range(3):
                zone = (dz, hz)
                base, rows = ZONE_BASE[zone], ZONE_ROWS[zone]
                filled = space[:, base : base + rows, :].astype(BF16)
                if zone in AHEAD:
                    send_buffers[zone][...] = filled
                    if zone not in LATER:
                        send_ahead(zone)
                else:
                    group = GROUP_LIST.index(((dz - 1), (hz - 1)))
                    x[2 * group : 2 * group + 2, 0:rows, :] = filled
    @pl.when(late == 0)
    def _():
        first_share().start()

    weight[...] = jnp.transpose(weight_t[...].astype(F32)).astype(BF16)
    grad[...] = jnp.zeros_like(grad)
    scale = HEAD**-0.5

    @pl.loop(0, 8)
    def _(turn):
        pair = turn // 2
        i = turn + late * pair * (3 - pair) * (3 - 2 * pair)
        for number, group in enumerate(GROUP_LIST):
            if number:

                @pl.when(i == 2 * number)
                def _():
                    for zone in GROUPS[group]:
                        if zone in AHEAD:
                            ahead(zone, 0).wait_recv()
                            ahead(zone, 1).wait_recv()

        @pl.when(turn == 0)
        def _():
            pass_on(DEEP[0])

        @pl.when(turn == 1)
        def _():
            for zone in LATER:
                send_ahead(zone)

        @pl.when(turn == 3)
        def _():
            pass_on(DEEP[1])

        @pl.when(turn == 3 + 2 * late)
        def _():
            first_share().wait_recv()

            @pl.when(lax.rem(depth, 4) == 1)
            def _():
                pass_share().start()

            @pl.loop(1, batches)
            def _(step):
                next_share(step).start()

        normed = x[i, :, 0:C]
        label_row = label[i]
        label_column = jnp.transpose(jnp.broadcast_to(label_row, (8, ROWS)))[:, 0:1]
        bias[...] = jnp.where(label_column == label_row, 0.0, -1e30)
        proj[...] = nn(normed, weight[...]).astype(BF16)
        proj_t[...] = nt(weight_t[...], normed).astype(BF16)
        dcon_t[...] = nt(eye[...], x[i, :, C:FEED]).astype(BF16)
        parts = [[slice(k * ATTN + h * HEAD, k * ATTN + h * HEAD + HEAD) for k in range(3)] for h in range(HEADS)]
        for head, (a, b, c) in enumerate(parts):
            score_all[head] = nn(proj[:, b], proj_t[a, :]) * (scale * math.log2(math.e)) + bias[...]
        for head, (a, b, c) in enumerate(parts):
            scores = score_all[head]
            exponent = jnp.exp2(scores - jnp.max(scores, axis=0, keepdims=True))
            weight_all[head] = (exponent * (1.0 / jnp.sum(exponent, axis=0, keepdims=True))).astype(BF16)
            con_t[a, :] = nn(proj_t[c, :], weight_all[head])
            cot = x[i, :, C + head * HEAD : C + head * HEAD + HEAD]
            dproj_t[c, :] = jnp.transpose(nn(weight_all[head], cot)).astype(BF16)
        for head, (a, b, c) in enumerate(parts):
            inner = jnp.sum(dcon_t[a, :].astype(F32) * con_t[a, :], axis=0, keepdims=True)
            dweights = nn(proj[:, c], dcon_t[a, :])
            dscore_all[head] = (weight_all[head].astype(F32) * (dweights - inner) * scale).astype(BF16)
        for head, (a, b, c) in enumerate(parts):
            dproj_t[a, :] = nn(proj_t[b, :], dscore_all[head]).astype(BF16)
            dproj_t[b, :] = jnp.transpose(nn(dscore_all[head], proj[:, a])).astype(BF16)
        context_w[i] = jnp.transpose(con_t[...]).astype(BF16)
        grad[...] += nn(dproj_t[...], normed)
        for number, group in enumerate(GROUP_LIST):
            if number:
                for half in range(2):

                    @pl.when(i == 2 * number + half)
                    def _():
                        for zone in GROUPS[group]:
                            if zone in AHEAD:
                                back(zone, half).start()

    def place_of(owner):
        return owner // heights % across, owner // heights // across * heights + owner % heights

    spread = jnp.transpose(grad[...])
    terms[0][...] = jnp.zeros_like(terms[0])
    for o in range(owners):
        terms[0][*place_of(o), 0:lines, 0 : 3 * ATTN] = spread[o * lines : (o + 1) * lines].astype(BF16)
    begin(0, 0)

    for zone in ZONES:
        if zone not in AHEAD:
            group = GROUP_LIST.index((zone[0] - 1, zone[1] - 1))
            base, rows = ZONE_BASE[zone], ZONE_ROWS[zone]
            context_z[:, base : base + rows, :] = context_w[2 * group : 2 * group + 2, 0:rows, :]
    context_space[:, TOTAL:, :] = jnp.zeros((2, context_space.shape[1] - TOTAL, ATTN), F32)

    def restore(dz):
        start, stop = ZONE_BASE[(dz, 0)], ZONE_BASE[(dz, 2)] + ZONE_ROWS[(dz, 2)]
        context_space[:, start:stop, :] = context_z[:, start:stop, :].astype(F32)
        for at in range(SIZES[dz]):
            d = FIRST[dz] + at
            pieces = []
            for half, hz, _ in PIECES:
                row = ZONE_BASE[(dz, hz)] + at * WIN * SIZES[hz]
                pieces.append(context_space[half, row : row + PIECE_ROWS[hz], :])
            context = nn(back_pick[...], jnp.concatenate(pieces, axis=0).astype(BF16))
            context_all[d * SLAB : (d + 1) * SLAB, :] = context.astype(BF16)

    for dz in (1, 2, 0):
        for zone in HALO:
            if zone[0] == dz:
                for half in range(2):
                    back(zone, half).wait_recv()
        restore(dz)

    grad_proj = tn(context_all[...], pad_u[...].reshape(EDGE * SLAB, C))
    terms[1][...] = jnp.zeros_like(terms[1])
    per = ATTN // owners
    for o in range(owners):
        rows = grad_proj[o * per : (o + 1) * per].astype(BF16)
        terms[1][*place_of(o), 0:per, 0:ATTN] = rows[:, 0:ATTN]
        terms[1][*place_of(o), per : 2 * per, 0:ATTN] = rows[:, ATTN:]
    begin(0, 1)

    def merge_pair(pair):
        blocks = []
        for d in (2 * pair, 2 * pair + 1):
            attended = nn(context_all[d * SLAB : (d + 1) * SLAB, :], weight_p[...]).astype(BF16)
            shown, hidden = masked_pick(cells[...], mask[d])
            tokens = nn(shown, pad_v[d].reshape(SLAB, C)) + hidden * token
            block = (tokens + nn(cells[...], attended)).astype(BF16).astype(F32)
            blocks += [block[o * 56 : o * 56 + 56] for o in range(4)]
        summed = sum(blocks[1:], blocks[0])
        mean = jnp.sum(summed, axis=1, keepdims=True) * (1.0 / (8 * C))
        centered = [b - mean for b in blocks]
        squares = [b * b for b in centered]
        variance = jnp.sum(sum(squares[1:], squares[0]), axis=1, keepdims=True) * (1.0 / (8 * C))
        factor = lax.rsqrt(variance + EPS)
        for o in range(8):
            features[o, pair * 56 : pair * 56 + 56, :] = centered[o] * factor * params[2 + o : 3 + o, :]

    for pair in range(4):
        merge_pair(pair)
    finish(0, 0)
    begin(1, 0)
    for pair in range(4, EDGE // 2):
        merge_pair(pair)
    finish(0, 1)
    begin(1, 1)

    @pl.loop(1, batches)
    def _(step):
        next_share(step).wait_recv()

    each = 8 // batches
    result = jnp.zeros(features.shape[1:], F32)
    for step in range(batches):
        at = lax.rem(batch - step + batches, batches) * each
        for k in range(each):
            result += nn(features[at + k].astype(BF16), other[step, k * C : (k + 1) * C, :])
    sent[0 : result.shape[0], :] = result.astype(BF16)
    sent[result.shape[0] :, :] = jnp.zeros((sent.shape[0] - result.shape[0], C), BF16)
    swap_merged().start()
    for kind in range(2):
        finish(1, kind)
        begin(2, kind)
    result = jnp.zeros(features.shape[1:], F32)
    for step in range(batches):
        for k in range(each):
            result += nn(features[step * each + k].astype(BF16), own[step, k * C : (k + 1) * C, :])
    merged_out[height] = result.astype(BF16)
    for kind in range(2):
        finish(2, kind)
    sums = partial[2]
    grad_qkv_out[...] = sums[0][0:lines, 0 : 3 * ATTN]
    grad_proj_out[:, 0:ATTN] = sums[1][0:per, 0:ATTN]
    grad_proj_out[:, ATTN:] = sums[1][per : 2 * per, 0:ATTN]
    swap_merged().wait_recv()
    merged_out[heights - 1 - height] = fetched[0 : result.shape[0], :]

    for zone in HALO:
        for half in range(2):
            ahead(zone, half).wait_send()
            back(zone, half).wait_send()
    if relayed:

        @pl.when(along == 3)
        def _():
            for zone in DEEP:
                from_relay(zone).wait_send()

    @pl.when(late == 0)
    def _():
        first_share().wait_send()

    @pl.when(lax.rem(depth, 4) == 1)
    def _():
        pass_share().wait_send()

    swap_merged().wait_send()

    @pl.loop(1, batches)
    def _(step):
        next_share(step).wait_send()

    for stage in range(3):
        for kind in range(2):

            @pl.loop(1, counts[stage])
            def _(step):
                exchange(stage, kind, step).wait_send()


def run_block(operands, sizes):
    vmem = pl.BlockSpec(memory_space=pltpu.VMEM)
    owners, batches = sizes[0] * sizes[1], sizes[2]
    lines = up(C // owners, 16)
    wide, narrow = up(3 * ATTN, 128), up(ATTN, 128)
    cell_rows = 7 * 56

    across = min(sizes[0], 4)
    planes = owners // across

    def pair_of(kind, *shape):
        return [pltpu.VMEM(shape + (lines, wide), kind), pltpu.VMEM(shape + (lines, narrow), kind)]

    exchanges = across + planes + batches

    return pl.pallas_call(
        functools.partial(block_kernel, sizes),
        out_shape=[
            jax.ShapeDtypeStruct((2, cell_rows, C), BF16),
            jax.ShapeDtypeStruct((C // owners, 3 * ATTN), F32),
            jax.ShapeDtypeStruct((ATTN // owners, C), F32),
        ],
        in_specs=[vmem] * len(operands),
        out_specs=[vmem] * 3,
        scratch_shapes=[
            pltpu.VMEM((8, ROWS, FEED), BF16),
            pltpu.VMEM((2, TOTAL, FEED), F32),
            pltpu.VMEM((EDGE, EDGE, PITCH, C), BF16),
            pltpu.VMEM((EDGE, EDGE, PITCH, C), BF16),
            pltpu.VMEM((8, ROWS, ATTN), BF16),
            pltpu.VMEM((2, TOTAL, ATTN), BF16),
            pltpu.VMEM((ROWS, ROWS), F32),
            pltpu.VMEM((ROWS, 3 * ATTN), BF16),
            pltpu.VMEM((3 * ATTN, ROWS), BF16),
            pltpu.VMEM((ATTN, ROWS), BF16),
            pltpu.VMEM((ATTN, ROWS), F32),
            pltpu.VMEM((3 * ATTN, ROWS), BF16),
            pltpu.VMEM((3 * ATTN, C), F32),
            pltpu.VMEM((2, TOTAL + 32, ATTN), F32),
            pltpu.VMEM((EDGE * SLAB, ATTN), BF16),
            pltpu.VMEM((8, cell_rows, C), F32),
            pltpu.VMEM((batches, 8 * C // batches, C), BF16),
            pltpu.VMEM((up(cell_rows, 16), C), BF16),
            pltpu.VMEM((up(cell_rows, 16), C), BF16),
            pair_of(BF16, across, planes),
            [pair_of(BF16, across, planes), pair_of(F32, planes), pair_of(F32, batches)],
            [pair_of(F32, planes), pair_of(F32), pair_of(F32)],
            pltpu.SemaphoreType.DMA((10,)),
            pltpu.SemaphoreType.DMA((10,)),
            pltpu.SemaphoreType.DMA((10,)),
            pltpu.SemaphoreType.DMA((10,)),
            pltpu.SemaphoreType.DMA((batches + 1,)),
            pltpu.SemaphoreType.DMA((batches,)),
            pltpu.SemaphoreType.DMA((1,)),
            pltpu.SemaphoreType.DMA((1,)),
            pltpu.SemaphoreType.DMA((2, exchanges)),
            pltpu.SemaphoreType.DMA((2, exchanges)),
        ]
        + [pltpu.VMEM((2, ZONE_ROWS[zone], FEED), BF16) for zone in HALO]
        + [
            pltpu.VMEM((HEADS, ROWS, ROWS), F32),
            pltpu.VMEM((HEADS, ROWS, ROWS), BF16),
            pltpu.VMEM((HEADS, ROWS, ROWS), BF16),
            pltpu.VMEM((C, 3 * ATTN), BF16),
            pltpu.SemaphoreType.DMA((2,)),
            pltpu.SemaphoreType.DMA((2,)),
        ]
        + [pltpu.VMEM((ZONE_ROWS[zone], FEED), BF16) for zone in DEEP],
        cost_estimate=pl.CostEstimate(flops=80_000_000_000, bytes_accessed=12_000_000, transcendentals=8_000_000),
        compiler_params=pltpu.CompilerParams(
            collective_id=1, has_side_effects=True, vmem_limit_bytes=VMEM_LIMIT
        ),
        name="block",
    )(*operands)


def group_labels(labels, group):
    parts = []
    for zone in GROUPS[group]:
        spans = []
        for z in zone:
            start = {1: 0, 2: WIN, 0: WIN + SIZES[2]}[z]
            spans.append((start, SIZES[z]))
        (d, nd), (h, nh) = spans
        part = labels[d : d + nd, h : h + nh].reshape(nd, nh, 2, WIN).transpose(2, 0, 1, 3)
        part = part.reshape(2, nd * nh * WIN)
        parts.append(jnp.pad(part, ((0, 0), (0, ZONE_ROWS[zone] - nd * nh * WIN)), constant_values=-1))
    row = jnp.concatenate(parts, axis=1)
    row = jnp.pad(row, ((0, 0), (0, ROWS - row.shape[1])), constant_values=-1)
    return row.reshape(2, 1, ROWS).astype(F32)


def shards(
    volume,
    patch_mask,
    mask_token,
    labels,
    norm_gain,
    qkv_weight,
    proj_weight,
    merge_gain,
    merge_weight,
    upstream,
):
    sizes = tuple(lax.axis_size(n) for n in ("depth", "height", "batch"))
    pick = slab_to_pieces()
    mask = jnp.pad(patch_mask[0], ((0, 0), (0, 0), (0, PITCH - EDGE))).reshape(EDGE, 1, SLAB).astype(BF16)
    label = jnp.concatenate([group_labels(labels[0], group) for group in GROUP_LIST], 0)
    params = jnp.concatenate((norm_gain, mask_token.astype(F32), merge_gain)).reshape(10, C)
    operands = (
        volume,
        upstream,
        mask,
        label,
        jnp.asarray(pick, BF16),
        jnp.asarray(pick.T, BF16),
        jnp.asarray(slab_to_cells(), BF16),
        params,
        qkv_weight.T,
        proj_weight,
        jnp.asarray(np.eye(ATTN), BF16),
        merge_weight.reshape(sizes[2], -1, C),
    )
    merged, grad_qkv, grad_proj = run_block(operands, sizes)
    merged = merged.reshape(2, 7, 7, 8, C)[:, :, :, :7].transpose(1, 0, 2, 3, 4).reshape(1, 7, 14, 7, C)
    return (merged, grad_qkv, grad_proj)


def solution(mesh):
    return jax.shard_map(
        shards,
        mesh=mesh,
        in_specs=(
            P("batch", "depth", "height", None, None),
            P("batch", "depth", "height", None),
            P(),
            P("batch", "depth", "height", None),
            P(),
            P(),
            P(),
            P(),
            P(None, "height"),
            P("batch", "depth", "height", None, None),
        ),
        out_specs=(
            P("batch", "depth", None, None, "height"),
            P(("depth", "height"), None),
            P(("depth", "height"), None),
        ),
        check_vma=False,
    )
```

```python
import functools
import math

import jax
import jax.numpy as jnp
import numpy as np
from jax import lax
from jax.experimental import pallas as pl
from jax.experimental.pallas import tpu as pltpu
from jax.sharding import PartitionSpec as P

HEADS = 6
HEAD = 32
ATTN = 192
C = 384
WIN = 7
SHIFT = 3
EDGE = 14
PITCH = 16
SLAB = EDGE * PITCH
ROWS = 384
FEED = C + ATTN
EPS = 1e-05
F32 = jnp.float32
BF16 = jnp.bfloat16
MESH = pl.DeviceIdType.MESH
VMEM_LIMIT = 58 * 2**20

SIZES = (3, 7, 4)
FIRST = (0, 3, 10)
ZONES = [(a, b) for a in range(3) for b in range(3)]


def up(value, unit):
    return -(-value // unit) * unit


ZONE_ROWS = {z: up(WIN * SIZES[z[0]] * SIZES[z[1]], 16) for z in ZONES}
ZONE_BASE = {}
TOTAL = 0
for zone in ZONES:
    ZONE_BASE[zone] = TOTAL
    TOTAL += ZONE_ROWS[zone]
PIECE_ROWS = tuple(up(WIN * s, 8) for s in SIZES)
PIECES = []
_at = 0
for _half in range(2):
    for _hz in range(3):
        PIECES.append((_half, _hz, _at))
        _at += PIECE_ROWS[_hz]

GROUPS = {
    (0, 0): ((1, 1),),
    (0, 1): ((1, 2), (1, 0)),
    (1, 0): ((2, 1), (0, 1)),
    (1, 1): ((2, 2), (2, 0), (0, 2), (0, 0)),
}


def slab_to_pieces():
    pick = np.zeros((SLAB, SLAB), np.float32)
    for half, hz, base in PIECES:
        for hh in range(SIZES[hz]):
            for k in range(WIN):
                width = (SHIFT + WIN * half + k) % EDGE
                pick[base + hh * WIN + k, (FIRST[hz] + hh) * PITCH + width] = 1
    return pick


def slab_to_cells():
    pick = np.zeros((SLAB, SLAB), np.float32)
    for hh in range(2):
        for ww in range(2):
            for h in range(7):
                for w in range(7):
                    pick[(hh * 2 + ww) * 56 + h * 8 + w, (2 * h + hh) * PITCH + 2 * w + ww] = 1
    return pick


def nn(a, b):
    return jnp.dot(a, b, preferred_element_type=F32)


def nt(a, b):
    return lax.dot_general(a, b, (((1,), (1,)), ((), ())), preferred_element_type=F32)


def tn(a, b):
    return lax.dot_general(a, b, (((0,), (0,)), ((), ())), preferred_element_type=F32)


def masked_pick(pick, mask_row):
    hidden = pick * mask_row
    return pick - hidden, jnp.sum(hidden.astype(F32), axis=1, keepdims=True)


AHEAD = {}
for _group, _members in GROUPS.items():
    _row = 0
    for zone in _members:
        if 0 in zone:
            AHEAD[zone] = (_group, _row)
        _row += ZONE_ROWS[zone]
HALO = list(AHEAD)
DEEP = [(0, 1), (0, 2)]
LATER = [(2, 0), (0, 2), (0, 0)]
GROUP_LIST = list(GROUPS)


def neighbour(zone, by, sizes):
    device = {}
    for axis, part, size in zip(("depth", "height"), zone, sizes):
        if part == 0:
            device[axis] = lax.rem(lax.axis_index(axis) + by + size, size)
    return device


def zone_of(d):
    dz = 0 if d < FIRST[1] else 1 if d < FIRST[2] else 2
    return dz, d - FIRST[dz]


def block_kernel(sizes, *refs):
    depths, heights, batches = sizes
    owners = depths * heights
    lines = C // owners
    vol, ups, mask, label, pick, back_pick, cells, params, weight_t, weight_p, eye, own = refs[:12]
    merged_out, grad_qkv_out, grad_proj_out = refs[12:15]
    x, space, pad_v, pad_u, context_w, context_z, bias, proj, proj_t, dcon_t, con_t, dproj_t = refs[15:27]
    grad, context_space, context_all, features, other, sent, fetched = refs[27:34]
    terms, landed, partial, ahead_send, ahead_recv, back_send, back_recv = refs[34:41]
    share_send, share_recv, merged_send, merged_recv, term_send, term_recv = refs[41:47]
    send_buffers = dict(zip(HALO, refs[47:52]))
    score_all, weight_all, dscore_all, weight, relay_send, relay_recv = refs[52:58]
    relay_buffers = dict(zip(DEEP, refs[58:60]))

    depth, height, batch = (lax.axis_index(n) for n in ("depth", "height", "batch"))
    me = depth * heights + height
    peer = {"height": heights - 1 - height}

    across = min(depths, 4)
    planes = owners // across
    across_at = lax.rem(depth, across)
    plane_at = depth // across * heights + height

    def owner_at(step):
        to = lax.rem(me + step, owners)
        return {"depth": to // heights, "height": lax.rem(to, heights)}

    cores = 2 - batches % 2
    lanes = batches // cores
    core, lane = lax.rem(batch, cores), batch // cores
    sibling = {"batch": lane * cores + cores - 1 - core}
    held = planes // cores
    holder = plane_at // held == core

    def lane_at(step):
        return {"batch": lax.rem(lane + step, lanes) * cores + core}

    def batch_at(step):
        return {"batch": lax.rem(batch + step, batches)}

    def remote(src, dst, send, recv, device):
        return pltpu.make_async_remote_copy(
            src_ref=src, dst_ref=dst, send_sem=send, recv_sem=recv, device_id=device, device_id_type=MESH
        )

    relayed = depths % 4 == 0 and depths > 4
    along = lax.rem(depth, 4)
    late = 1 - (along + 3) // 4

    def landing(zone, half):
        group, row = AHEAD[zone]
        return x.at[2 * GROUP_LIST.index(group) + half, pl.ds(row, ZONE_ROWS[zone]), :]

    def ahead(zone, half):
        slot = 2 * HALO.index(zone) + half
        return remote(
            send_buffers[zone].at[half],
            landing(zone, half),
            ahead_send.at[slot],
            ahead_recv.at[slot],
            neighbour(zone, -1, sizes),
        )

    def to_relay(zone):
        slot = DEEP.index(zone)
        return remote(
            send_buffers[zone].at[1],
            relay_buffers[zone],
            ahead_send.at[2 * HALO.index(zone) + 1],
            relay_recv.at[slot],
            {"depth": lax.rem(depth + 3, depths)},
        )

    def from_relay(zone):
        return remote(
            relay_buffers[zone],
            landing(zone, 1),
            relay_send.at[DEEP.index(zone)],
            ahead_recv.at[2 * HALO.index(zone) + 1],
            {"depth": lax.rem(depth + depths - 4, depths)},
        )

    def send_ahead(zone):
        ahead(zone, 0).start()
        if relayed and zone in DEEP:

            @pl.when(late == 1)
            def _():
                to_relay(zone).start()

            @pl.when(late == 0)
            def _():
                ahead(zone, 1).start()
        else:
            ahead(zone, 1).start()

    def pass_on(zone):
        if relayed:

            @pl.when(along == 3)
            def _():
                to_relay(zone).wait_recv()
                from_relay(zone).start()

    def back(zone, half):
        group, row = AHEAD[zone]
        slot = 2 * HALO.index(zone) + half
        return remote(
            context_w.at[2 * GROUP_LIST.index(group) + half, pl.ds(row, ZONE_ROWS[zone]), :],
            context_z.at[half, pl.ds(ZONE_BASE[zone], ZONE_ROWS[zone]), :],
            back_send.at[slot],
            back_recv.at[slot],
            neighbour(zone, 1, sizes),
        )

    def first_share():
        return remote(own.at[batch], other.at[0], share_send.at[0], share_recv.at[0], peer)

    def pass_share():
        before = {"depth": lax.rem(depth + depths - 1, depths)}
        return remote(other.at[0], other.at[0], share_send.at[batches], share_recv.at[0], before)

    def next_share(step):
        place = other.at[step * cores]
        return remote(other.at[0], place, share_send.at[step], share_recv.at[step], lane_at(step))

    def twin_share(step):
        source, slot = other.at[step * cores], lanes + step
        return remote(source, other.at[step * cores + 1], share_send.at[slot], share_recv.at[slot], sibling)

    def swap_merged():
        return remote(sent, fetched, merged_send.at[0], merged_recv.at[0], peer)

    paired, from_x, from_z, from_y = landed
    chip, x_sum, z_sum, final = partial
    base_y = across + planes

    def slot_of(kind, slot):
        return term_send.at[kind, slot], term_recv.at[kind, slot]

    def to_twin(kind):
        return remote(terms[kind].at[cores - 1 - core], paired[kind], *slot_of(kind, 0), sibling)

    def to_x(kind, step):
        place = lax.rem(across_at + step, across)
        device = {"depth": depth // across * across + place}
        return remote(chip[kind].at[place], from_x[kind].at[step], *slot_of(kind, step), device)

    def to_z(kind, step):
        plane = lax.rem(plane_at + step, planes)
        device = {"depth": plane // heights * across + across_at, "height": lax.rem(plane, heights)}
        source = x_sum[kind].at[lax.rem(plane, held)]
        return remote(source, from_z[kind].at[step], *slot_of(kind, across + step), device)

    def to_y(kind, step):
        return remote(z_sum[kind], from_y[kind].at[step], *slot_of(kind, base_y + step), lane_at(step))

    def to_other_core(kind):
        return remote(final[kind], final[kind], *slot_of(kind, base_y), sibling)

    def sends_z(step):
        return lax.rem(plane_at + step, planes) // held == core

    def begin_twin(kind):
        if cores == 2:
            to_twin(kind).start()

    def begin_x(kind):
        if cores == 2:
            to_twin(kind).wait_recv()
            chip[kind][...] = (terms[kind][core] + paired[kind][...]).astype(BF16)
        else:
            chip[kind][...] = terms[kind][0].astype(BF16)

        @pl.loop(1, across)
        def _(step):
            to_x(kind, step).start()

    def begin_z(kind):
        x_sum[kind][...] = chip[kind][across_at].astype(F32)

        @pl.loop(1, across)
        def _(step):
            to_x(kind, step).wait_recv()
            x_sum[kind][...] += from_x[kind][step].astype(F32)

        @pl.loop(1, planes)
        def _(step):
            @pl.when(sends_z(step))
            def _():
                to_z(kind, step).start()

    def begin_y(kind):
        @pl.when(holder)
        def _():
            z_sum[kind][...] = x_sum[kind][lax.rem(plane_at, held)]

            @pl.loop(1, planes)
            def _(step):
                to_z(kind, step).wait_recv()
                z_sum[kind][...] += from_z[kind][step]

            @pl.loop(1, lanes)
            def _(step):
                to_y(kind, step).start()

    def begin_last(kind):
        @pl.when(holder)
        def _():
            final[kind][...] = z_sum[kind][...]

            @pl.loop(1, lanes)
            def _(step):
                to_y(kind, step).wait_recv()
                final[kind][...] += from_y[kind][step]

            if cores == 2:
                to_other_core(kind).start()

    def finish(kind):
        if cores == 2:

            @pl.when(jnp.logical_not(holder))
            def _():
                to_other_core(kind).wait_recv()

    def settle(kind):
        if cores == 2:
            to_twin(kind).wait_send()

        @pl.loop(1, across)
        def _(step):
            to_x(kind, step).wait_send()

        @pl.loop(1, planes)
        def _(step):
            @pl.when(sends_z(step))
            def _():
                to_z(kind, step).wait_send()

        @pl.when(holder)
        def _():
            @pl.loop(1, lanes)
            def _(step):
                to_y(kind, step).wait_send()

            if cores == 2:
                to_other_core(kind).wait_send()

    barrier = pltpu.get_barrier_semaphore()

    @pl.loop(1, owners)
    def _(step):
        pl.semaphore_signal(barrier, inc=1, device_id=owner_at(step), device_id_type=MESH)

    @pl.loop(1, batches)
    def _(step):
        pl.semaphore_signal(barrier, inc=1, device_id=batch_at(step), device_id_type=MESH)

    gain, token = params[0:1, :], params[1:2, :]
    space[...] = jnp.zeros_like(space)
    pad_v[...] = jnp.zeros_like(pad_v)
    pad_u[...] = jnp.zeros_like(pad_u)
    for number, group in enumerate(GROUP_LIST):
        used = sum(ZONE_ROWS[zone] for zone in GROUPS[group])
        x[2 * number : 2 * number + 2, used:, :] = jnp.zeros((2, ROWS - used, FEED), BF16)
    for d in range(EDGE):
        dz, at = zone_of(d)
        for h in range(EDGE):
            pad_v[d, h, 0:EDGE, :] = vol[0, d, h]
            pad_u[d, h, 0:EDGE, :] = ups[0, d, h]
        shown, hidden = masked_pick(pick[...], mask[d])
        tokens = nn(shown, pad_v[d].reshape(SLAB, C)) + hidden * token
        mean = jnp.mean(tokens, axis=1, keepdims=True)
        centered = tokens - mean
        variance = jnp.mean(centered * centered, axis=1, keepdims=True)
        normed = centered * lax.rsqrt(variance + EPS) * gain
        dcontext = nt(nn(pick[...], pad_u[d].reshape(SLAB, C)).astype(BF16), weight_p[...])
        for half, hz, base in PIECES:
            size = WIN * SIZES[hz]
            row = ZONE_BASE[(dz, hz)] + at * size
            space[half, row : row + size, 0:C] = normed[base : base + size]
            space[half, row : row + size, C:FEED] = dcontext[base : base + size]
        if at == SIZES[dz] - 1:
            if dz == 0:
                pl.semaphore_wait(barrier, owners + batches - 2)
            for hz in range(3):
                zone = (dz, hz)
                base, rows = ZONE_BASE[zone], ZONE_ROWS[zone]
                filled = space[:, base : base + rows, :].astype(BF16)
                if zone in AHEAD:
                    send_buffers[zone][...] = filled
                    if zone not in LATER:
                        send_ahead(zone)
                else:
                    group = GROUP_LIST.index(((dz - 1), (hz - 1)))
                    x[2 * group : 2 * group + 2, 0:rows, :] = filled
    @pl.when(late == 0)
    def _():
        first_share().start()

    weight[...] = jnp.transpose(weight_t[...].astype(F32)).astype(BF16)
    grad[...] = jnp.zeros_like(grad)
    scale = HEAD**-0.5

    @pl.loop(0, 8)
    def _(turn):
        pair = turn // 2
        i = turn + late * pair * (3 - pair) * (3 - 2 * pair)
        for number, group in enumerate(GROUP_LIST):
            if number:

                @pl.when(i == 2 * number)
                def _():
                    for zone in GROUPS[group]:
                        if zone in AHEAD:
                            ahead(zone, 0).wait_recv()
                            ahead(zone, 1).wait_recv()

        @pl.when(turn == 0)
        def _():
            pass_on(DEEP[0])

        @pl.when(turn == 1)
        def _():
            for zone in LATER:
                send_ahead(zone)

        @pl.when(turn == 3)
        def _():
            pass_on(DEEP[1])

        @pl.when(turn == 2 + 2 * late)
        def _():
            first_share().wait_recv()

            @pl.when(lax.rem(depth, 4) == 1)
            def _():
                pass_share().start()

            if cores == 2:
                twin_share(0).start()

            @pl.loop(1, lanes)
            def _(step):
                next_share(step).start()

        normed = x[i, :, 0:C]
        label_row = label[i]
        label_column = jnp.transpose(jnp.broadcast_to(label_row, (8, ROWS)))[:, 0:1]
        bias[...] = jnp.where(label_column == label_row, 0.0, -1e30)
        proj[...] = nn(normed, weight[...]).astype(BF16)
        proj_t[...] = nt(weight_t[...], normed).astype(BF16)
        dcon_t[...] = nt(eye[...], x[i, :, C:FEED]).astype(BF16)
        parts = [[slice(k * ATTN + h * HEAD, k * ATTN + h * HEAD + HEAD) for k in range(3)] for h in range(HEADS)]
        for head, (a, b, c) in enumerate(parts):
            score_all[head] = nn(proj[:, b], proj_t[a, :]) * (scale * math.log2(math.e)) + bias[...]
        for head, (a, b, c) in enumerate(parts):
            scores = score_all[head]
            exponent = jnp.exp2(scores - jnp.max(scores, axis=0, keepdims=True))
            weight_all[head] = (exponent * (1.0 / jnp.sum(exponent, axis=0, keepdims=True))).astype(BF16)
            con_t[a, :] = nn(proj_t[c, :], weight_all[head])
            cot = x[i, :, C + head * HEAD : C + head * HEAD + HEAD]
            dproj_t[c, :] = jnp.transpose(nn(weight_all[head], cot)).astype(BF16)
        for head, (a, b, c) in enumerate(parts):
            inner = jnp.sum(dcon_t[a, :].astype(F32) * con_t[a, :], axis=0, keepdims=True)
            dweights = nn(proj[:, c], dcon_t[a, :])
            dscore_all[head] = (weight_all[head].astype(F32) * (dweights - inner) * scale).astype(BF16)
        for head, (a, b, c) in enumerate(parts):
            dproj_t[a, :] = nn(proj_t[b, :], dscore_all[head]).astype(BF16)
            dproj_t[b, :] = jnp.transpose(nn(dscore_all[head], proj[:, a])).astype(BF16)
        context_w[i] = jnp.transpose(con_t[...]).astype(BF16)
        grad[...] += nn(dproj_t[...], normed)
        for number, group in enumerate(GROUP_LIST):
            if number:
                for half in range(2):

                    @pl.when(i == 2 * number + half)
                    def _():
                        for zone in GROUPS[group]:
                            if zone in AHEAD:
                                back(zone, half).start()

    def place_of(owner):
        plane = owner // heights // across * heights + owner % heights
        return plane // held, owner // heights % across, plane % held

    spread = jnp.transpose(grad[...])
    terms[0][...] = jnp.zeros_like(terms[0])
    for o in range(owners):
        terms[0][*place_of(o), 0:lines, 0 : 3 * ATTN] = spread[o * lines : (o + 1) * lines]
    begin_twin(0)

    @pl.loop(1, lanes)
    def _(step):
        next_share(step).wait_recv()
        if cores == 2:
            twin_share(step).start()

    for zone in ZONES:
        if zone not in AHEAD:
            group = GROUP_LIST.index((zone[0] - 1, zone[1] - 1))
            base, rows = ZONE_BASE[zone], ZONE_ROWS[zone]
            context_z[:, base : base + rows, :] = context_w[2 * group : 2 * group + 2, 0:rows, :]
    context_space[:, TOTAL:, :] = jnp.zeros((2, context_space.shape[1] - TOTAL, ATTN), F32)

    def restore(dz):
        start, stop = ZONE_BASE[(dz, 0)], ZONE_BASE[(dz, 2)] + ZONE_ROWS[(dz, 2)]
        context_space[:, start:stop, :] = context_z[:, start:stop, :].astype(F32)
        for at in range(SIZES[dz]):
            d = FIRST[dz] + at
            pieces = []
            for half, hz, _ in PIECES:
                row = ZONE_BASE[(dz, hz)] + at * WIN * SIZES[hz]
                pieces.append(context_space[half, row : row + PIECE_ROWS[hz], :])
            context = nn(back_pick[...], jnp.concatenate(pieces, axis=0).astype(BF16))
            context_all[d * SLAB : (d + 1) * SLAB, :] = context.astype(BF16)

    for dz in (1, 2, 0):
        for zone in HALO:
            if zone[0] == dz:
                for half in range(2):
                    back(zone, half).wait_recv()
        restore(dz)
        if dz == 1:
            begin_x(0)

    grad_proj = tn(context_all[...], pad_u[...].reshape(EDGE * SLAB, C))
    terms[1][...] = jnp.zeros_like(terms[1])
    per = ATTN // owners
    for o in range(owners):
        rows = grad_proj[o * per : (o + 1) * per]
        terms[1][*place_of(o), 0:per, 0:ATTN] = rows[:, 0:ATTN]
        terms[1][*place_of(o), per : 2 * per, 0:ATTN] = rows[:, ATTN:]
    begin_twin(1)

    def merge_pair(pair):
        blocks = []
        for d in (2 * pair, 2 * pair + 1):
            attended = nn(context_all[d * SLAB : (d + 1) * SLAB, :], weight_p[...]).astype(BF16)
            shown, hidden = masked_pick(cells[...], mask[d])
            tokens = nn(shown, pad_v[d].reshape(SLAB, C)) + hidden * token
            block = (tokens + nn(cells[...], attended)).astype(BF16).astype(F32)
            blocks += [block[o * 56 : o * 56 + 56] for o in range(4)]
        summed = sum(blocks[1:], blocks[0])
        mean = jnp.sum(summed, axis=1, keepdims=True) * (1.0 / (8 * C))
        centered = [b - mean for b in blocks]
        squares = [b * b for b in centered]
        variance = jnp.sum(sum(squares[1:], squares[0]), axis=1, keepdims=True) * (1.0 / (8 * C))
        factor = lax.rsqrt(variance + EPS)
        for o in range(8):
            features[o, pair * 56 : pair * 56 + 56, :] = centered[o] * factor * params[2 + o : 3 + o, :]

    for pair in range(EDGE // 2):
        merge_pair(pair)
        if pair == 1:
            begin_x(1)
        if pair == 4:
            begin_z(0)
    begin_z(1)
    if cores == 2:

        @pl.loop(0, lanes)
        def _(step):
            twin_share(step).wait_recv()

    each = 8 // batches
    result = jnp.zeros(features.shape[1:], F32)
    for step in range(batches):
        crop = lax.rem(lane - step // cores + lanes, lanes) * cores
        at = (crop + (core if step % cores == 0 else cores - 1 - core)) * each
        for k in range(each):
            result += nn(features[at + k].astype(BF16), other[step, k * C : (k + 1) * C, :])
    sent[0 : result.shape[0], :] = result.astype(BF16)
    sent[result.shape[0] :, :] = jnp.zeros((sent.shape[0] - result.shape[0], C), BF16)
    swap_merged().start()
    begin_y(0)
    begin_y(1)
    result = jnp.zeros(features.shape[1:], F32)
    for step in range(batches):
        for k in range(each):
            result += nn(features[step * each + k].astype(BF16), own[step, k * C : (k + 1) * C, :])
    merged_out[height] = result.astype(BF16)
    begin_last(0)
    begin_last(1)
    swap_merged().wait_recv()
    merged_out[heights - 1 - height] = fetched[0 : result.shape[0], :]
    finish(0)
    finish(1)
    grad_qkv_out[...] = final[0][0:lines, 0 : 3 * ATTN]
    grad_proj_out[:, 0:ATTN] = final[1][0:per, 0:ATTN]
    grad_proj_out[:, ATTN:] = final[1][per : 2 * per, 0:ATTN]

    for zone in HALO:
        for half in range(2):
            ahead(zone, half).wait_send()
            back(zone, half).wait_send()
    if relayed:

        @pl.when(along == 3)
        def _():
            for zone in DEEP:
                from_relay(zone).wait_send()

    @pl.when(late == 0)
    def _():
        first_share().wait_send()

    @pl.when(lax.rem(depth, 4) == 1)
    def _():
        pass_share().wait_send()

    swap_merged().wait_send()

    @pl.loop(1, lanes)
    def _(step):
        next_share(step).wait_send()

    if cores == 2:

        @pl.loop(0, lanes)
        def _(step):
            twin_share(step).wait_send()

    settle(0)
    settle(1)


def run_block(operands, sizes):
    vmem = pl.BlockSpec(memory_space=pltpu.VMEM)
    owners, batches = sizes[0] * sizes[1], sizes[2]
    lines = up(C // owners, 16)
    wide, narrow = up(3 * ATTN, 128), up(ATTN, 128)
    cell_rows = 7 * 56

    across = min(sizes[0], 4)
    planes = owners // across

    def pair_of(kind, *shape):
        return [pltpu.VMEM(shape + (lines, wide), kind), pltpu.VMEM(shape + (lines, narrow), kind)]

    cores = 2 - batches % 2
    held = planes // cores
    exchanges = across + planes + batches // cores

    return pl.pallas_call(
        functools.partial(block_kernel, sizes),
        out_shape=[
            jax.ShapeDtypeStruct((2, cell_rows, C), BF16),
            jax.ShapeDtypeStruct((C // owners, 3 * ATTN), F32),
            jax.ShapeDtypeStruct((ATTN // owners, C), F32),
        ],
        in_specs=[vmem] * len(operands),
        out_specs=[vmem] * 3,
        scratch_shapes=[
            pltpu.VMEM((8, ROWS, FEED), BF16),
            pltpu.VMEM((2, TOTAL, FEED), F32),
            pltpu.VMEM((EDGE, EDGE, PITCH, C), BF16),
            pltpu.VMEM((EDGE, EDGE, PITCH, C), BF16),
            pltpu.VMEM((8, ROWS, ATTN), BF16),
            pltpu.VMEM((2, TOTAL, ATTN), BF16),
            pltpu.VMEM((ROWS, ROWS), F32),
            pltpu.VMEM((ROWS, 3 * ATTN), BF16),
            pltpu.VMEM((3 * ATTN, ROWS), BF16),
            pltpu.VMEM((ATTN, ROWS), BF16),
            pltpu.VMEM((ATTN, ROWS), F32),
            pltpu.VMEM((3 * ATTN, ROWS), BF16),
            pltpu.VMEM((3 * ATTN, C), F32),
            pltpu.VMEM((2, TOTAL + 32, ATTN), F32),
            pltpu.VMEM((EDGE * SLAB, ATTN), BF16),
            pltpu.VMEM((8, cell_rows, C), F32),
            pltpu.VMEM((batches, 8 * C // batches, C), BF16),
            pltpu.VMEM((up(cell_rows, 16), C), BF16),
            pltpu.VMEM((up(cell_rows, 16), C), BF16),
            pair_of(F32, cores, across, held),
            [
                pair_of(F32, across, held),
                pair_of(BF16, across, held),
                pair_of(F32, planes),
                pair_of(F32, batches // cores),
            ],
            [pair_of(BF16, across, held), pair_of(F32, held), pair_of(F32), pair_of(F32)],
            pltpu.SemaphoreType.DMA((10,)),
            pltpu.SemaphoreType.DMA((10,)),
            pltpu.SemaphoreType.DMA((10,)),
            pltpu.SemaphoreType.DMA((10,)),
            pltpu.SemaphoreType.DMA((batches + 1,)),
            pltpu.SemaphoreType.DMA((batches,)),
            pltpu.SemaphoreType.DMA((1,)),
            pltpu.SemaphoreType.DMA((1,)),
            pltpu.SemaphoreType.DMA((2, exchanges)),
            pltpu.SemaphoreType.DMA((2, exchanges)),
        ]
        + [pltpu.VMEM((2, ZONE_ROWS[zone], FEED), BF16) for zone in HALO]
        + [
            pltpu.VMEM((HEADS, ROWS, ROWS), F32),
            pltpu.VMEM((HEADS, ROWS, ROWS), BF16),
            pltpu.VMEM((HEADS, ROWS, ROWS), BF16),
            pltpu.VMEM((C, 3 * ATTN), BF16),
            pltpu.SemaphoreType.DMA((2,)),
            pltpu.SemaphoreType.DMA((2,)),
        ]
        + [pltpu.VMEM((ZONE_ROWS[zone], FEED), BF16) for zone in DEEP],
        cost_estimate=pl.CostEstimate(flops=80_000_000_000, bytes_accessed=12_000_000, transcendentals=8_000_000),
        compiler_params=pltpu.CompilerParams(
            collective_id=1, has_side_effects=True, vmem_limit_bytes=VMEM_LIMIT
        ),
        name="block",
    )(*operands)


def group_labels(labels, group):
    parts = []
    for zone in GROUPS[group]:
        spans = []
        for z in zone:
            start = {1: 0, 2: WIN, 0: WIN + SIZES[2]}[z]
            spans.append((start, SIZES[z]))
        (d, nd), (h, nh) = spans
        part = labels[d : d + nd, h : h + nh].reshape(nd, nh, 2, WIN).transpose(2, 0, 1, 3)
        part = part.reshape(2, nd * nh * WIN)
        parts.append(jnp.pad(part, ((0, 0), (0, ZONE_ROWS[zone] - nd * nh * WIN)), constant_values=-1))
    row = jnp.concatenate(parts, axis=1)
    row = jnp.pad(row, ((0, 0), (0, ROWS - row.shape[1])), constant_values=-1)
    return row.reshape(2, 1, ROWS).astype(F32)


def shards(
    volume,
    patch_mask,
    mask_token,
    labels,
    norm_gain,
    qkv_weight,
    proj_weight,
    merge_gain,
    merge_weight,
    upstream,
):
    sizes = tuple(lax.axis_size(n) for n in ("depth", "height", "batch"))
    pick = slab_to_pieces()
    mask = jnp.pad(patch_mask[0], ((0, 0), (0, 0), (0, PITCH - EDGE))).reshape(EDGE, 1, SLAB).astype(BF16)
    label = jnp.concatenate([group_labels(labels[0], group) for group in GROUP_LIST], 0)
    params = jnp.concatenate((norm_gain, mask_token.astype(F32), merge_gain)).reshape(10, C)
    operands = (
        volume,
        upstream,
        mask,
        label,
        jnp.asarray(pick, BF16),
        jnp.asarray(pick.T, BF16),
        jnp.asarray(slab_to_cells(), BF16),
        params,
        qkv_weight.T,
        proj_weight,
        jnp.asarray(np.eye(ATTN), BF16),
        merge_weight.reshape(sizes[2], -1, C),
    )
    merged, grad_qkv, grad_proj = run_block(operands, sizes)
    merged = merged.reshape(2, 7, 7, 8, C)[:, :, :, :7].transpose(1, 0, 2, 3, 4).reshape(1, 7, 14, 7, C)
    return (merged, grad_qkv, grad_proj)


def solution(mesh):
    return jax.shard_map(
        shards,
        mesh=mesh,
        in_specs=(
            P("batch", "depth", "height", None, None),
            P("batch", "depth", "height", None),
            P(),
            P("batch", "depth", "height", None),
            P(),
            P(),
            P(),
            P(),
            P(None, "height"),
            P("batch", "depth", "height", None, None),
        ),
        out_specs=(
            P("batch", "depth", None, None, "height"),
            P(("depth", "height"), None),
            P(("depth", "height"), None),
        ),
        check_vma=False,
    )
```

```python
import functools
import math

import jax
import jax.numpy as jnp
import numpy as np
from jax import lax
from jax.experimental import pallas as pl
from jax.experimental.pallas import tpu as pltpu
from jax.sharding import PartitionSpec as P

HEADS = 6
HEAD = 32
ATTN = 192
C = 384
WIN = 7
SHIFT = 3
EDGE = 14
PITCH = 16
SLAB = EDGE * PITCH
ROWS = 384
FEED = C + ATTN
EPS = 1e-05
F32 = jnp.float32
BF16 = jnp.bfloat16
MESH = pl.DeviceIdType.MESH
VMEM_LIMIT = 58 * 2**20

SIZES = (3, 7, 4)
FIRST = (0, 3, 10)
ZONES = [(a, b) for a in range(3) for b in range(3)]


def up(value, unit):
    return -(-value // unit) * unit


ZONE_ROWS = {z: up(WIN * SIZES[z[0]] * SIZES[z[1]], 16) for z in ZONES}
ZONE_BASE = {}
TOTAL = 0
for zone in ZONES:
    ZONE_BASE[zone] = TOTAL
    TOTAL += ZONE_ROWS[zone]
PIECE_ROWS = tuple(up(WIN * s, 8) for s in SIZES)
PIECES = []
_at = 0
for _half in range(2):
    for _hz in range(3):
        PIECES.append((_half, _hz, _at))
        _at += PIECE_ROWS[_hz]

GROUPS = {
    (0, 0): ((1, 1),),
    (0, 1): ((1, 2), (1, 0)),
    (1, 0): ((2, 1), (0, 1)),
    (1, 1): ((2, 2), (2, 0), (0, 2), (0, 0)),
}


def slab_to_pieces():
    pick = np.zeros((SLAB, SLAB), np.float32)
    for half, hz, base in PIECES:
        for hh in range(SIZES[hz]):
            for k in range(WIN):
                width = (SHIFT + WIN * half + k) % EDGE
                pick[base + hh * WIN + k, (FIRST[hz] + hh) * PITCH + width] = 1
    return pick


def slab_to_cells():
    pick = np.zeros((SLAB, SLAB), np.float32)
    for hh in range(2):
        for ww in range(2):
            for h in range(7):
                for w in range(7):
                    pick[(hh * 2 + ww) * 56 + h * 8 + w, (2 * h + hh) * PITCH + 2 * w + ww] = 1
    return pick


def nn(a, b):
    return jnp.dot(a, b, preferred_element_type=F32)


def nt(a, b):
    return lax.dot_general(a, b, (((1,), (1,)), ((), ())), preferred_element_type=F32)


def tn(a, b):
    return lax.dot_general(a, b, (((0,), (0,)), ((), ())), preferred_element_type=F32)


def masked_pick(pick, mask_row):
    hidden = pick * mask_row
    return pick - hidden, jnp.sum(hidden.astype(F32), axis=1, keepdims=True)


AHEAD = {}
for _group, _members in GROUPS.items():
    _row = 0
    for zone in _members:
        if 0 in zone:
            AHEAD[zone] = (_group, _row)
        _row += ZONE_ROWS[zone]
HALO = list(AHEAD)
DEEP = {((0, 1), 0): 1, ((0, 1), 1): 3, ((0, 2), 0): 2}
LATER = [(2, 0), (0, 2), (0, 0)]
GROUP_LIST = list(GROUPS)


def neighbour(zone, by, sizes):
    device = {}
    for axis, part, size in zip(("depth", "height"), zone, sizes):
        if part == 0:
            device[axis] = lax.rem(lax.axis_index(axis) + by + size, size)
    return device


def zone_of(d):
    dz = 0 if d < FIRST[1] else 1 if d < FIRST[2] else 2
    return dz, d - FIRST[dz]


def block_kernel(sizes, *refs):
    depths, heights, batches = sizes
    owners = depths * heights
    lines = C // owners
    vol, ups, mask, label, pick, back_pick, cells, params, weight_t, weight_p, eye, own = refs[:12]
    merged_out, grad_qkv_out, grad_proj_out = refs[12:15]
    x, space, pad_v, pad_u, context_w, context_z, bias, proj, proj_t, dcon_t, con_t, dproj_t = refs[15:27]
    grad, context_space, context_all, features, other, sent, fetched = refs[27:34]
    terms, landed, partial, ahead_send, ahead_recv, back_send, back_recv = refs[34:41]
    share_send, share_recv, merged_send, merged_recv, term_send, term_recv = refs[41:47]
    send_buffers = dict(zip(HALO, refs[47:52]))
    score_all, weight_all, dscore_all, weight, relay_send, relay_recv = refs[52:58]
    relay_buffers = dict(zip(DEEP, refs[58:61]))

    depth, height, batch = (lax.axis_index(n) for n in ("depth", "height", "batch"))
    me = depth * heights + height
    peer = {"height": heights - 1 - height}

    across = min(depths, 4)
    planes = owners // across
    across_at = lax.rem(depth, across)
    plane_at = depth // across * heights + height

    def owner_at(step):
        to = lax.rem(me + step, owners)
        return {"depth": to // heights, "height": lax.rem(to, heights)}

    cores = 2 - batches % 2
    lanes = batches // cores
    core, lane = lax.rem(batch, cores), batch // cores
    sibling = {"batch": lane * cores + cores - 1 - core}
    held = planes // cores
    holder = plane_at // held == core

    def lane_at(step):
        return {"batch": lax.rem(lane + step, lanes) * cores + core}

    def batch_at(step):
        return {"batch": lax.rem(batch + step, batches)}

    def remote(src, dst, send, recv, device):
        return pltpu.make_async_remote_copy(
            src_ref=src, dst_ref=dst, send_sem=send, recv_sem=recv, device_id=device, device_id_type=MESH
        )

    relayed = depths % 4 == 0 and depths > 4
    along = lax.rem(depth, 4)
    late = 1 - (along + 3) // 4

    def landing(zone, half):
        group, row = AHEAD[zone]
        return x.at[2 * GROUP_LIST.index(group) + half, pl.ds(row, ZONE_ROWS[zone]), :]

    def ahead(zone, half):
        slot = 2 * HALO.index(zone) + half
        return remote(
            send_buffers[zone].at[half],
            landing(zone, half),
            ahead_send.at[slot],
            ahead_recv.at[slot],
            neighbour(zone, -1, sizes),
        )

    def to_relay(piece):
        zone, half = piece
        return remote(
            send_buffers[zone].at[half],
            relay_buffers[piece],
            ahead_send.at[2 * HALO.index(zone) + half],
            relay_recv.at[list(DEEP).index(piece)],
            {"depth": lax.rem(depth + DEEP[piece], depths)},
        )

    def from_relay(piece):
        zone, half = piece
        return remote(
            relay_buffers[piece],
            landing(zone, half),
            relay_send.at[list(DEEP).index(piece)],
            ahead_recv.at[2 * HALO.index(zone) + half],
            {"depth": lax.rem(depth + depths - 1 - DEEP[piece], depths)},
        )

    def send_ahead(zone):
        for half in range(2):
            if relayed and (zone, half) in DEEP:

                @pl.when(late == 1)
                def _():
                    to_relay((zone, half)).start()

                @pl.when(late == 0)
                def _():
                    ahead(zone, half).start()
            else:
                ahead(zone, half).start()

    def pass_on(zone):
        for piece, place in DEEP.items():
            if relayed and piece[0] == zone:

                @pl.when(along == place)
                def _():
                    to_relay(piece).wait_recv()
                    from_relay(piece).start()

    def back(zone, half):
        group, row = AHEAD[zone]
        slot = 2 * HALO.index(zone) + half
        return remote(
            context_w.at[2 * GROUP_LIST.index(group) + half, pl.ds(row, ZONE_ROWS[zone]), :],
            context_z.at[half, pl.ds(ZONE_BASE[zone], ZONE_ROWS[zone]), :],
            back_send.at[slot],
            back_recv.at[slot],
            neighbour(zone, 1, sizes),
        )

    def first_share():
        return remote(own.at[batch], other.at[0], share_send.at[0], share_recv.at[0], peer)

    def pass_share():
        before = {"depth": lax.rem(depth + depths - 1, depths)}
        return remote(other.at[0], other.at[0], share_send.at[batches], share_recv.at[0], before)

    def next_share(step):
        place = other.at[step * cores]
        return remote(other.at[0], place, share_send.at[step], share_recv.at[step], lane_at(step))

    def twin_share(step):
        source, slot = other.at[step * cores], lanes + step
        return remote(source, other.at[step * cores + 1], share_send.at[slot], share_recv.at[slot], sibling)

    def swap_merged():
        return remote(sent, fetched, merged_send.at[0], merged_recv.at[0], peer)

    paired, from_x, from_z, from_y = landed
    chip, x_sum, z_sum, final = partial
    base_y = across + planes

    def slot_of(kind, slot):
        return term_send.at[kind, slot], term_recv.at[kind, slot]

    def to_twin(kind):
        return remote(terms[kind].at[cores - 1 - core], paired[kind], *slot_of(kind, 0), sibling)

    def to_x(kind, step):
        place = lax.rem(across_at + step, across)
        device = {"depth": depth // across * across + place}
        return remote(chip[kind].at[place], from_x[kind].at[step], *slot_of(kind, step), device)

    def to_z(kind, step):
        plane = lax.rem(plane_at + step, planes)
        device = {"depth": plane // heights * across + across_at, "height": lax.rem(plane, heights)}
        source = x_sum[kind].at[lax.rem(plane, held)]
        return remote(source, from_z[kind].at[step], *slot_of(kind, across + step), device)

    def to_y(kind, step):
        return remote(z_sum[kind], from_y[kind].at[step], *slot_of(kind, base_y + step), lane_at(step))

    def to_other_core(kind):
        return remote(final[kind], final[kind], *slot_of(kind, base_y), sibling)

    def sends_z(step):
        return lax.rem(plane_at + step, planes) // held == core

    def begin_twin(kind):
        if cores == 2:
            to_twin(kind).start()

    def begin_x(kind):
        if cores == 2:
            to_twin(kind).wait_recv()
            chip[kind][...] = (terms[kind][core] + paired[kind][...]).astype(BF16)
        else:
            chip[kind][...] = terms[kind][0].astype(BF16)

        @pl.loop(1, across)
        def _(step):
            to_x(kind, step).start()

    def begin_z(kind):
        x_sum[kind][...] = chip[kind][across_at].astype(F32)

        @pl.loop(1, across)
        def _(step):
            to_x(kind, step).wait_recv()
            x_sum[kind][...] += from_x[kind][step].astype(F32)

        @pl.loop(1, planes)
        def _(step):
            @pl.when(sends_z(step))
            def _():
                to_z(kind, step).start()

    def begin_y(kind):
        @pl.when(holder)
        def _():
            z_sum[kind][...] = x_sum[kind][lax.rem(plane_at, held)]

            @pl.loop(1, planes)
            def _(step):
                to_z(kind, step).wait_recv()
                z_sum[kind][...] += from_z[kind][step]

            @pl.loop(1, lanes)
            def _(step):
                to_y(kind, step).start()

    def begin_last(kind):
        @pl.when(holder)
        def _():
            final[kind][...] = z_sum[kind][...]

            @pl.loop(1, lanes)
            def _(step):
                to_y(kind, step).wait_recv()
                final[kind][...] += from_y[kind][step]

            if cores == 2:
                to_other_core(kind).start()

    def finish(kind):
        if cores == 2:

            @pl.when(jnp.logical_not(holder))
            def _():
                to_other_core(kind).wait_recv()

    def settle(kind):
        if cores == 2:
            to_twin(kind).wait_send()

        @pl.loop(1, across)
        def _(step):
            to_x(kind, step).wait_send()

        @pl.loop(1, planes)
        def _(step):
            @pl.when(sends_z(step))
            def _():
                to_z(kind, step).wait_send()

        @pl.when(holder)
        def _():
            @pl.loop(1, lanes)
            def _(step):
                to_y(kind, step).wait_send()

            if cores == 2:
                to_other_core(kind).wait_send()

    barrier = pltpu.get_barrier_semaphore()

    @pl.loop(1, owners)
    def _(step):
        pl.semaphore_signal(barrier, inc=1, device_id=owner_at(step), device_id_type=MESH)

    @pl.loop(1, batches)
    def _(step):
        pl.semaphore_signal(barrier, inc=1, device_id=batch_at(step), device_id_type=MESH)

    gain, token = params[0:1, :], params[1:2, :]
    space[...] = jnp.zeros_like(space)
    pad_v[...] = jnp.zeros_like(pad_v)
    pad_u[...] = jnp.zeros_like(pad_u)
    for number, group in enumerate(GROUP_LIST):
        used = sum(ZONE_ROWS[zone] for zone in GROUPS[group])
        x[2 * number : 2 * number + 2, used:, :] = jnp.zeros((2, ROWS - used, FEED), BF16)
    for d in range(EDGE):
        dz, at = zone_of(d)
        for h in range(EDGE):
            pad_v[d, h, 0:EDGE, :] = vol[0, d, h]
            pad_u[d, h, 0:EDGE, :] = ups[0, d, h]
        shown, hidden = masked_pick(pick[...], mask[d])
        tokens = nn(shown, pad_v[d].reshape(SLAB, C)) + hidden * token
        mean = jnp.mean(tokens, axis=1, keepdims=True)
        centered = tokens - mean
        variance = jnp.mean(centered * centered, axis=1, keepdims=True)
        normed = centered * lax.rsqrt(variance + EPS) * gain
        dcontext = nt(nn(pick[...], pad_u[d].reshape(SLAB, C)).astype(BF16), weight_p[...])
        for half, hz, base in PIECES:
            size = WIN * SIZES[hz]
            row = ZONE_BASE[(dz, hz)] + at * size
            space[half, row : row + size, 0:C] = normed[base : base + size]
            space[half, row : row + size, C:FEED] = dcontext[base : base + size]
        if at == SIZES[dz] - 1:
            if dz == 0:
                pl.semaphore_wait(barrier, owners + batches - 2)
            for hz in range(3):
                zone = (dz, hz)
                base, rows = ZONE_BASE[zone], ZONE_ROWS[zone]
                filled = space[:, base : base + rows, :].astype(BF16)
                if zone in AHEAD:
                    send_buffers[zone][...] = filled
                    if zone not in LATER:
                        send_ahead(zone)
                else:
                    group = GROUP_LIST.index(((dz - 1), (hz - 1)))
                    x[2 * group : 2 * group + 2, 0:rows, :] = filled
    @pl.when(late == 0)
    def _():
        first_share().start()

    weight[...] = jnp.transpose(weight_t[...].astype(F32)).astype(BF16)
    grad[...] = jnp.zeros_like(grad)
    scale = HEAD**-0.5

    @pl.loop(0, 8)
    def _(turn):
        pair = turn // 2
        i = turn + late * pair * (3 - pair) * (3 - 2 * pair)
        for number, group in enumerate(GROUP_LIST):
            if number:

                @pl.when(i == 2 * number)
                def _():
                    for zone in GROUPS[group]:
                        if zone in AHEAD:
                            ahead(zone, 0).wait_recv()
                            ahead(zone, 1).wait_recv()

        @pl.when(turn == 0)
        def _():
            pass_on((0, 1))

        @pl.when(turn == 1)
        def _():
            for zone in LATER:
                send_ahead(zone)

        @pl.when(turn == 3)
        def _():
            pass_on((0, 2))

        @pl.when(turn == 2 + 2 * late)
        def _():
            first_share().wait_recv()

            @pl.when(lax.rem(depth, 4) == 1)
            def _():
                pass_share().start()

            if cores == 2:
                twin_share(0).start()

            @pl.loop(1, lanes)
            def _(step):
                next_share(step).start()

        normed = x[i, :, 0:C]
        label_row = label[i]
        label_column = jnp.transpose(jnp.broadcast_to(label_row, (8, ROWS)))[:, 0:1]
        bias[...] = jnp.where(label_column == label_row, 0.0, -1e30)
        proj[...] = nn(normed, weight[...]).astype(BF16)
        proj_t[...] = nt(weight_t[...], normed).astype(BF16)
        dcon_t[...] = nt(eye[...], x[i, :, C:FEED]).astype(BF16)
        parts = [[slice(k * ATTN + h * HEAD, k * ATTN + h * HEAD + HEAD) for k in range(3)] for h in range(HEADS)]
        for head, (a, b, c) in enumerate(parts):
            score_all[head] = nn(proj[:, b], proj_t[a, :]) * (scale * math.log2(math.e)) + bias[...]
        for head, (a, b, c) in enumerate(parts):
            scores = score_all[head]
            exponent = jnp.exp2(scores - jnp.max(scores, axis=0, keepdims=True))
            weight_all[head] = (exponent * (1.0 / jnp.sum(exponent, axis=0, keepdims=True))).astype(BF16)
            con_t[a, :] = nn(proj_t[c, :], weight_all[head])
            cot = x[i, :, C + head * HEAD : C + head * HEAD + HEAD]
            dproj_t[c, :] = jnp.transpose(nn(weight_all[head], cot)).astype(BF16)
        for head, (a, b, c) in enumerate(parts):
            inner = jnp.sum(dcon_t[a, :].astype(F32) * con_t[a, :], axis=0, keepdims=True)
            dweights = nn(proj[:, c], dcon_t[a, :])
            dscore_all[head] = (weight_all[head].astype(F32) * (dweights - inner) * scale).astype(BF16)
        for head, (a, b, c) in enumerate(parts):
            dproj_t[a, :] = nn(proj_t[b, :], dscore_all[head]).astype(BF16)
            dproj_t[b, :] = jnp.transpose(nn(dscore_all[head], proj[:, a])).astype(BF16)
        context_w[i] = jnp.transpose(con_t[...]).astype(BF16)
        grad[...] += nn(dproj_t[...], normed)
        for number, group in enumerate(GROUP_LIST):
            if number:
                for half in range(2):

                    @pl.when(i == 2 * number + half)
                    def _():
                        for zone in GROUPS[group]:
                            if zone in AHEAD:
                                back(zone, half).start()

    def place_of(owner):
        plane = owner // heights // across * heights + owner % heights
        return plane // held, owner // heights % across, plane % held

    spread = jnp.transpose(grad[...])
    terms[0][...] = jnp.zeros_like(terms[0])
    for o in range(owners):
        terms[0][*place_of(o), 0:lines, 0 : 3 * ATTN] = spread[o * lines : (o + 1) * lines]
    begin_twin(0)

    @pl.loop(1, lanes)
    def _(step):
        next_share(step).wait_recv()
        if cores == 2:
            twin_share(step).start()

    for zone in ZONES:
        if zone not in AHEAD:
            group = GROUP_LIST.index((zone[0] - 1, zone[1] - 1))
            base, rows = ZONE_BASE[zone], ZONE_ROWS[zone]
            context_z[:, base : base + rows, :] = context_w[2 * group : 2 * group + 2, 0:rows, :]
    context_space[:, TOTAL:, :] = jnp.zeros((2, context_space.shape[1] - TOTAL, ATTN), F32)

    def restore(dz):
        start, stop = ZONE_BASE[(dz, 0)], ZONE_BASE[(dz, 2)] + ZONE_ROWS[(dz, 2)]
        context_space[:, start:stop, :] = context_z[:, start:stop, :].astype(F32)
        for at in range(SIZES[dz]):
            d = FIRST[dz] + at
            pieces = []
            for half, hz, _ in PIECES:
                row = ZONE_BASE[(dz, hz)] + at * WIN * SIZES[hz]
                pieces.append(context_space[half, row : row + PIECE_ROWS[hz], :])
            context = nn(back_pick[...], jnp.concatenate(pieces, axis=0).astype(BF16))
            context_all[d * SLAB : (d + 1) * SLAB, :] = context.astype(BF16)

    for dz in (1, 2, 0):
        for zone in HALO:
            if zone[0] == dz:
                for half in range(2):
                    back(zone, half).wait_recv()
        restore(dz)
        if dz == 1:
            begin_x(0)

    grad_proj = tn(context_all[...], pad_u[...].reshape(EDGE * SLAB, C))
    terms[1][...] = jnp.zeros_like(terms[1])
    per = ATTN // owners
    for o in range(owners):
        rows = grad_proj[o * per : (o + 1) * per]
        terms[1][*place_of(o), 0:per, 0:ATTN] = rows[:, 0:ATTN]
        terms[1][*place_of(o), per : 2 * per, 0:ATTN] = rows[:, ATTN:]
    begin_twin(1)

    def merge_pair(pair):
        blocks = []
        for d in (2 * pair, 2 * pair + 1):
            attended = nn(context_all[d * SLAB : (d + 1) * SLAB, :], weight_p[...]).astype(BF16)
            shown, hidden = masked_pick(cells[...], mask[d])
            tokens = nn(shown, pad_v[d].reshape(SLAB, C)) + hidden * token
            block = (tokens + nn(cells[...], attended)).astype(BF16).astype(F32)
            blocks += [block[o * 56 : o * 56 + 56] for o in range(4)]
        summed = sum(blocks[1:], blocks[0])
        mean = jnp.sum(summed, axis=1, keepdims=True) * (1.0 / (8 * C))
        centered = [b - mean for b in blocks]
        squares = [b * b for b in centered]
        variance = jnp.sum(sum(squares[1:], squares[0]), axis=1, keepdims=True) * (1.0 / (8 * C))
        factor = lax.rsqrt(variance + EPS)
        for o in range(8):
            features[o, pair * 56 : pair * 56 + 56, :] = centered[o] * factor * params[2 + o : 3 + o, :]

    for pair in range(EDGE // 2):
        merge_pair(pair)
        if pair == 1:
            begin_x(1)
        if pair == 4:
            begin_z(0)
    begin_z(1)
    if cores == 2:

        @pl.loop(0, lanes)
        def _(step):
            twin_share(step).wait_recv()

    each = 8 // batches
    result = jnp.zeros(features.shape[1:], F32)
    for step in range(batches):
        crop = lax.rem(lane - step // cores + lanes, lanes) * cores
        at = (crop + (core if step % cores == 0 else cores - 1 - core)) * each
        for k in range(each):
            result += nn(features[at + k].astype(BF16), other[step, k * C : (k + 1) * C, :])
    sent[0 : result.shape[0], :] = result.astype(BF16)
    sent[result.shape[0] :, :] = jnp.zeros((sent.shape[0] - result.shape[0], C), BF16)
    swap_merged().start()
    begin_y(0)
    begin_y(1)
    result = jnp.zeros(features.shape[1:], F32)
    for step in range(batches):
        for k in range(each):
            result += nn(features[step * each + k].astype(BF16), own[step, k * C : (k + 1) * C, :])
    merged_out[height] = result.astype(BF16)
    begin_last(0)
    begin_last(1)
    swap_merged().wait_recv()
    merged_out[heights - 1 - height] = fetched[0 : result.shape[0], :]
    finish(0)
    finish(1)
    grad_qkv_out[...] = final[0][0:lines, 0 : 3 * ATTN]
    grad_proj_out[:, 0:ATTN] = final[1][0:per, 0:ATTN]
    grad_proj_out[:, ATTN:] = final[1][per : 2 * per, 0:ATTN]

    for zone in HALO:
        for half in range(2):
            ahead(zone, half).wait_send()
            back(zone, half).wait_send()
    if relayed:

        for piece, place in DEEP.items():

            @pl.when(along == place)
            def _():
                from_relay(piece).wait_send()

    @pl.when(late == 0)
    def _():
        first_share().wait_send()

    @pl.when(lax.rem(depth, 4) == 1)
    def _():
        pass_share().wait_send()

    swap_merged().wait_send()

    @pl.loop(1, lanes)
    def _(step):
        next_share(step).wait_send()

    if cores == 2:

        @pl.loop(0, lanes)
        def _(step):
            twin_share(step).wait_send()

    settle(0)
    settle(1)


def run_block(operands, sizes):
    vmem = pl.BlockSpec(memory_space=pltpu.VMEM)
    owners, batches = sizes[0] * sizes[1], sizes[2]
    lines = up(C // owners, 16)
    wide, narrow = up(3 * ATTN, 128), up(ATTN, 128)
    cell_rows = 7 * 56

    across = min(sizes[0], 4)
    planes = owners // across

    def pair_of(kind, *shape):
        return [pltpu.VMEM(shape + (lines, wide), kind), pltpu.VMEM(shape + (lines, narrow), kind)]

    cores = 2 - batches % 2
    held = planes // cores
    exchanges = across + planes + batches // cores

    return pl.pallas_call(
        functools.partial(block_kernel, sizes),
        out_shape=[
            jax.ShapeDtypeStruct((2, cell_rows, C), BF16),
            jax.ShapeDtypeStruct((C // owners, 3 * ATTN), F32),
            jax.ShapeDtypeStruct((ATTN // owners, C), F32),
        ],
        in_specs=[vmem] * len(operands),
        out_specs=[vmem] * 3,
        scratch_shapes=[
            pltpu.VMEM((8, ROWS, FEED), BF16),
            pltpu.VMEM((2, TOTAL, FEED), F32),
            pltpu.VMEM((EDGE, EDGE, PITCH, C), BF16),
            pltpu.VMEM((EDGE, EDGE, PITCH, C), BF16),
            pltpu.VMEM((8, ROWS, ATTN), BF16),
            pltpu.VMEM((2, TOTAL, ATTN), BF16),
            pltpu.VMEM((ROWS, ROWS), F32),
            pltpu.VMEM((ROWS, 3 * ATTN), BF16),
            pltpu.VMEM((3 * ATTN, ROWS), BF16),
            pltpu.VMEM((ATTN, ROWS), BF16),
            pltpu.VMEM((ATTN, ROWS), F32),
            pltpu.VMEM((3 * ATTN, ROWS), BF16),
            pltpu.VMEM((3 * ATTN, C), F32),
            pltpu.VMEM((2, TOTAL + 32, ATTN), F32),
            pltpu.VMEM((EDGE * SLAB, ATTN), BF16),
            pltpu.VMEM((8, cell_rows, C), F32),
            pltpu.VMEM((batches, 8 * C // batches, C), BF16),
            pltpu.VMEM((up(cell_rows, 16), C), BF16),
            pltpu.VMEM((up(cell_rows, 16), C), BF16),
            pair_of(F32, cores, across, held),
            [
                pair_of(F32, across, held),
                pair_of(BF16, across, held),
                pair_of(F32, planes),
                pair_of(F32, batches // cores),
            ],
            [pair_of(BF16, across, held), pair_of(F32, held), pair_of(F32), pair_of(F32)],
            pltpu.SemaphoreType.DMA((10,)),
            pltpu.SemaphoreType.DMA((10,)),
            pltpu.SemaphoreType.DMA((10,)),
            pltpu.SemaphoreType.DMA((10,)),
            pltpu.SemaphoreType.DMA((batches + 1,)),
            pltpu.SemaphoreType.DMA((batches,)),
            pltpu.SemaphoreType.DMA((1,)),
            pltpu.SemaphoreType.DMA((1,)),
            pltpu.SemaphoreType.DMA((2, exchanges)),
            pltpu.SemaphoreType.DMA((2, exchanges)),
        ]
        + [pltpu.VMEM((2, ZONE_ROWS[zone], FEED), BF16) for zone in HALO]
        + [
            pltpu.VMEM((HEADS, ROWS, ROWS), F32),
            pltpu.VMEM((HEADS, ROWS, ROWS), BF16),
            pltpu.VMEM((HEADS, ROWS, ROWS), BF16),
            pltpu.VMEM((C, 3 * ATTN), BF16),
            pltpu.SemaphoreType.DMA((3,)),
            pltpu.SemaphoreType.DMA((3,)),
        ]
        + [pltpu.VMEM((ZONE_ROWS[zone], FEED), BF16) for zone, _ in DEEP],
        cost_estimate=pl.CostEstimate(flops=80_000_000_000, bytes_accessed=12_000_000, transcendentals=8_000_000),
        compiler_params=pltpu.CompilerParams(
            collective_id=1, has_side_effects=True, vmem_limit_bytes=VMEM_LIMIT
        ),
        name="block",
    )(*operands)


def group_labels(labels, group):
    parts = []
    for zone in GROUPS[group]:
        spans = []
        for z in zone:
            start = {1: 0, 2: WIN, 0: WIN + SIZES[2]}[z]
            spans.append((start, SIZES[z]))
        (d, nd), (h, nh) = spans
        part = labels[d : d + nd, h : h + nh].reshape(nd, nh, 2, WIN).transpose(2, 0, 1, 3)
        part = part.reshape(2, nd * nh * WIN)
        parts.append(jnp.pad(part, ((0, 0), (0, ZONE_ROWS[zone] - nd * nh * WIN)), constant_values=-1))
    row = jnp.concatenate(parts, axis=1)
    row = jnp.pad(row, ((0, 0), (0, ROWS - row.shape[1])), constant_values=-1)
    return row.reshape(2, 1, ROWS).astype(F32)


def shards(
    volume,
    patch_mask,
    mask_token,
    labels,
    norm_gain,
    qkv_weight,
    proj_weight,
    merge_gain,
    merge_weight,
    upstream,
):
    sizes = tuple(lax.axis_size(n) for n in ("depth", "height", "batch"))
    pick = slab_to_pieces()
    mask = jnp.pad(patch_mask[0], ((0, 0), (0, 0), (0, PITCH - EDGE))).reshape(EDGE, 1, SLAB).astype(BF16)
    label = jnp.concatenate([group_labels(labels[0], group) for group in GROUP_LIST], 0)
    params = jnp.concatenate((norm_gain, mask_token.astype(F32), merge_gain)).reshape(10, C)
    operands = (
        volume,
        upstream,
        mask,
        label,
        jnp.asarray(pick, BF16),
        jnp.asarray(pick.T, BF16),
        jnp.asarray(slab_to_cells(), BF16),
        params,
        qkv_weight.T,
        proj_weight,
        jnp.asarray(np.eye(ATTN), BF16),
        merge_weight.reshape(sizes[2], -1, C),
    )
    merged, grad_qkv, grad_proj = run_block(operands, sizes)
    merged = merged.reshape(2, 7, 7, 8, C)[:, :, :, :7].transpose(1, 0, 2, 3, 4).reshape(1, 7, 14, 7, C)
    return (merged, grad_qkv, grad_proj)


def solution(mesh):
    return jax.shard_map(
        shards,
        mesh=mesh,
        in_specs=(
            P("batch", "depth", "height", None, None),
            P("batch", "depth", "height", None),
            P(),
            P("batch", "depth", "height", None),
            P(),
            P(),
            P(),
            P(),
            P(None, "height"),
            P("batch", "depth", "height", None, None),
        ),
        out_specs=(
            P("batch", "depth", None, None, "height"),
            P(("depth", "height"), None),
            P(("depth", "height"), None),
        ),
        check_vma=False,
    )
```
